512 devices in a mesh: dp: 64 (over y, z_lo, core), span: 8 (over x, z_hi).
Axes of the slice: x: 4, y: 4, z: 16 (z_hi: 2, z_lo: 8; z = z_hi * 8 + z_lo), core: 2. Of those that a mesh axis runs over, the one named last changes fastest.
Arguments:
- visual_tower_outputs: bfloat16 [131072, 1152], P(('dp', 'span')), may hold values from -6 to 6
- language_tower_outputs: bfloat16 [131072, 1152], P(('dp', 'span')), may hold values from -24 to 24
- visual_mapping_frozen: bfloat16 [1152, 768], replicated, may hold values from -0.1875 to 0.1875
- language_mapping_learnable: bfloat16 [1152, 768], replicated, may hold values from -0.1875 to 0.1875
- sigmoid_sharpness_array: float32 [1], replicated, may hold values from 30 to 100
- sigmoid_offset_array: float32 [1], replicated, may hold values from -8 to -2
Outputs:
- text_grad: bfloat16 [131072, 1152], P(('dp', 'span'))
- head_grad: float32 [1152, 768], P('dp', 'span')
The draws below stay inside these ranges and needn't reach their ends.
All inputs are finite; a program needn't handle non-finite values.
Results may differ from the reference program's by a relative error of at most 0.012.
Values may be sent and summed in bfloat16 or wider, within the bound.
No kernel may reach another device: no remote copies, remote signals or barrier semaphores. Data moves between devices by JAX's collectives and lax.ppermute only.
A program may use at most 64 MiB of HBM per device.

```python
import math
import jax
import jax.numpy as jnp
from jax import lax

FEAT = 1152
EMBED = 768
PAIRS_DEV = 256
PAIRS = 131072
N_DP = 64
N_SPAN = 8


def with_spikes(entries, key, source, target, parts, factor):
    def block_of(dim):
        return (jnp.arange(entries.shape[dim]) // (entries.shape[dim] // parts)).reshape((-1,) + (1,) * (entries.ndim - 1 - dim))

    one_side = jax.random.permutation(key, parts)[block_of(target)]
    second = (block_of(target) + parts // 2) % parts
    return jnp.where((block_of(source) == one_side) | (block_of(source) == second), factor * entries, entries)


def block_levels(own_key, dims, shards, least, high):
    gain, own = 1.0, jax.random.fold_in(own_key, 6)
    for position, blocks in shards:
        steps = jnp.exp(jax.random.uniform(jax.random.fold_in(own, position), (blocks,), jnp.float32, least / len(shards), high / len(shards)))
        gain = gain * jnp.repeat(steps, dims[position] // blocks).reshape([-1 if axis == position else 1 for axis in range(len(dims))])
    return gain


def noise(own_key, extent, deviation, limit, pieces=(), kind=jnp.bfloat16):
    level = block_levels(own_key, extent, pieces, -0.22, 0.18) if pieces else 1.0
    result = jax.random.normal(own_key, extent, jnp.float32) * deviation * level
    return jnp.minimum(jnp.maximum(result, -limit), limit).astype(kind)


def gaussian_with(rng, dims, spread, most, cuts, heavy, kind=jnp.bfloat16):
    values = spread * jax.random.normal(rng, dims, jnp.float32)
    if cuts:
        values = values * block_levels(rng, dims, cuts, -0.22, 0.18)
    return jnp.clip(with_spikes(values, jax.random.fold_in(rng, 3), *heavy), -most, most).astype(kind)


def setup_inputs(seed: int = 0) -> dict:
    key_of = jax.random.split(jax.random.key(seed), 7)
    return {
        "visual_tower_outputs": noise(key_of[0], (PAIRS, FEAT), 1.0, 6.0, ((0, 512),)),
        "language_tower_outputs": gaussian_with(key_of[1], (PAIRS, FEAT), 1.0, 24.0, ((0, 512),), (0, 1, 128, 5.5)),
        "visual_mapping_frozen": noise(key_of[2], (FEAT, EMBED), FEAT ** -0.5, 0.1875),
        "language_mapping_learnable": noise(key_of[3], (FEAT, EMBED), FEAT ** -0.5, 0.1875),
        "sigmoid_sharpness_array": jnp.clip(jnp.exp(jax.random.uniform(key_of[4], (1,), jnp.float32, math.log(30.0), math.log(100.0))), 30.0, 100.0),
        "sigmoid_offset_array": jnp.clip(jax.random.uniform(key_of[5], (1,), jnp.float32, -8.0, -2.0), -8.0, -2.0),
    }


EPSILON = 1e-06

def embed(feats, head):
    raw = jnp.dot(feats, head, preferred_element_type=jnp.float32)
    inverse = lax.rsqrt(lax.optimization_barrier(jnp.sum(raw * raw, axis=-1, keepdims=True)) + EPSILON)
    return (raw * inverse, inverse)

def reference(visual_tower_outputs, language_tower_outputs, visual_mapping_frozen, language_mapping_learnable, sigmoid_sharpness_array, sigmoid_offset_array):
    video_unit, unused_inv = embed(visual_tower_outputs, visual_mapping_frozen)
    video_emb = video_unit.astype(jnp.bfloat16)
    text_unit, text_inv = embed(language_tower_outputs, language_mapping_learnable)
    text_emb = text_unit.astype(jnp.bfloat16)
    reciprocal_sharpness = sigmoid_sharpness_array[0]
    sigmoid_additive_offset = sigmoid_offset_array[0]
    group_rows = PAIRS_DEV * N_SPAN
    video_groups = video_emb.reshape(N_DP, group_rows, EMBED)
    text_groups = text_emb.reshape(N_DP, group_rows, EMBED)

    def one_group(operands):
        visual_block_piece, language_block_piece = operands
        similarity_matrix = reciprocal_sharpness * jnp.dot(language_block_piece, visual_block_piece.T, preferred_element_type=jnp.float32) + sigmoid_additive_offset
        positions = jnp.arange(group_rows, dtype=jnp.int32)
        target_sign = jnp.where(positions[:, None] == positions[None, :], 1.0, -1.0).astype(jnp.float32)
        mapping_matrix = (-target_sign * jax.nn.sigmoid(-target_sign * similarity_matrix)).astype(jnp.bfloat16)
        return reciprocal_sharpness * jnp.dot(mapping_matrix, visual_block_piece, preferred_element_type=jnp.float32)
    caption_vector_derivative_matrix = lax.map(one_group, (video_groups, text_groups)).reshape(text_emb.shape[0], EMBED)
    inner = lax.optimization_barrier(jnp.sum(text_unit * caption_vector_derivative_matrix, axis=-1, keepdims=True))
    raw_grad = (text_inv * (caption_vector_derivative_matrix - text_unit * inner)).astype(jnp.bfloat16)
    text_grad = lax.dot_general(raw_grad, language_mapping_learnable, (((1,), (1,)), ((), ())), preferred_element_type=jnp.float32).astype(jnp.bfloat16)
    head_total = lax.dot_general(language_tower_outputs, raw_grad, (((0,), (0,)), ((), ())), preferred_element_type=jnp.float32)
    head_grad = head_total / jnp.float32(N_DP * N_SPAN)
    return (text_grad, head_grad)
```

```python
import jax
import jax.numpy as jnp
from jax import lax
from jax.sharding import Mesh, PartitionSpec as P

EPSILON = 1e-06
AXES = ("y", "zl", "c", "x", "zh")
SIZES = (4, 8, 2, 4, 2)


def ring(n, step):
    return [(i, (i + step) % n) for i in range(n)]


def embed(feats, head):
    raw = jnp.dot(feats, head, preferred_element_type=jnp.float32)
    inverse = lax.rsqrt(jnp.sum(raw * raw, axis=-1, keepdims=True) + EPSILON)
    return (raw * inverse, inverse)


def local(
    visual_tower_outputs,
    language_tower_outputs,
    visual_mapping_frozen,
    language_mapping_learnable,
    sigmoid_sharpness_array,
    sigmoid_offset_array,
):
    rows, feat = language_tower_outputs.shape
    width = visual_mapping_frozen.shape[1]
    ny, nzl, nc, nx, nzh = SIZES
    devices = ny * nzl * nc * nx * nzh
    piece_r = feat // (ny * nzl * nc)
    piece_c = width // (nx * nzh)
    sharp = sigmoid_sharpness_array[0]
    offset = sigmoid_offset_array[0]
    core = lax.axis_index("c")

    video_unit, unused_inv = embed(visual_tower_outputs, visual_mapping_frozen)
    video_emb = video_unit.astype(jnp.bfloat16)
    across = lax.ppermute(video_emb, "zh", ring(2, 1))
    near = [video_emb] + [lax.ppermute(video_emb, "x", ring(nx, k)) for k in (1, 3, 2)]
    far = [across] + [lax.ppermute(across, "x", ring(nx, k)) for k in (1, 3, 2)]

    text_unit, text_inv = embed(language_tower_outputs, language_mapping_learnable)
    text_emb = text_unit.astype(jnp.bfloat16)

    half = feat // 2
    place = lax.broadcasted_iota(jnp.int32, (half, feat), 0)
    source = lax.broadcasted_iota(jnp.int32, (half, feat), 1)
    start = (place // piece_r) * (2 * piece_r) + place % piece_r

    def columns_of(which):
        pick = (source == start + which * piece_r).astype(jnp.bfloat16)
        return lax.dot_general(
            pick, language_tower_outputs, (((1,), (1,)), ((), ())), preferred_element_type=jnp.float32
        ).astype(jnp.bfloat16)

    mine = columns_of(core)
    theirs = lax.ppermute(columns_of(1 - core), "c", ring(2, 1))

    def part(block, with_diagonal):
        scores = sharp * lax.dot_general(
            text_emb, block, (((1,), (1,)), ((), ())), preferred_element_type=jnp.float32
        ) + offset
        if with_diagonal:
            row = lax.broadcasted_iota(jnp.int32, scores.shape, 0)
            col = lax.broadcasted_iota(jnp.int32, scores.shape, 1)
            sign = jnp.where(row == col, 1.0, -1.0).astype(jnp.float32)
            weight = -sign * jax.nn.sigmoid(-sign * scores)
        else:
            weight = jax.nn.sigmoid(scores)
        return jnp.dot(weight.astype(jnp.bfloat16), block, preferred_element_type=jnp.float32)

    emb_grad = part(jnp.concatenate(near), True)
    emb_grad = sharp * (emb_grad + part(jnp.concatenate(far), False))
    inner = jnp.sum(text_unit * emb_grad, axis=-1, keepdims=True)
    raw_grad = (text_inv * (emb_grad - text_unit * inner)).astype(jnp.bfloat16)

    other = lax.ppermute(raw_grad, "c", ring(2, 1))
    text_grad = lax.dot_general(
        raw_grad, language_mapping_learnable, (((1,), (1,)), ((), ())), preferred_element_type=jnp.float32
    ).astype(jnp.bfloat16)

    term = jnp.dot(mine, raw_grad, preferred_element_type=jnp.float32) + jnp.dot(
        theirs, other, preferred_element_type=jnp.float32
    )
    block_r, block_c = nzl * piece_r, nzh * piece_c
    term = term.astype(jnp.bfloat16).reshape(ny, block_r, nx, block_c).transpose(0, 2, 1, 3)
    term = term.reshape(ny * nx, block_r, block_c)
    term = lax.all_to_all(term, ("y", "x"), 0, 0, tiled=True)
    term = jnp.sum(term.astype(jnp.float32), axis=0).astype(jnp.bfloat16)
    term = term.reshape(nzl, piece_r, nzh, piece_c).transpose(0, 2, 1, 3)
    term = term.reshape(nzl * nzh, piece_r, piece_c)
    term = lax.all_to_all(term, ("zl", "zh"), 0, 0, tiled=True)
    head_grad = jnp.sum(term.astype(jnp.float32), axis=0) / jnp.float32(devices)
    return (text_grad, head_grad)


def solution(mesh):
    fine = Mesh(mesh.devices.reshape(SIZES), AXES)
    pairs = P(("y", "zl", "c", "x", "zh"), None)
    return jax.shard_map(
        local,
        mesh=fine,
        in_specs=(pairs, pairs, P(), P(), P(), P()),
        out_specs=(pairs, P(("y", "zl", "c"), ("x", "zh"))),
        check_vma=False,
    )
```

```python
import jax
import jax.numpy as jnp
from jax import lax
from jax.experimental import pallas as pl
from jax.experimental.pallas import tpu as pltpu
from jax.sharding import Mesh, PartitionSpec as P

EPSILON = 1e-06
AXES = ("y", "zl", "c", "x", "zh")
SIZES = (4, 8, 2, 4, 2)
F32 = jnp.float32
BF16 = jnp.bfloat16
VMEM = pl.BlockSpec(memory_space=pltpu.VMEM)
SMEM = pl.BlockSpec(memory_space=pltpu.SMEM)
NT = (((1,), (1,)), ((), ()))


def ring(n, step):
    return [(i, (i + step) % n) for i in range(n)]


def call(kernel, outs, specs, flops, scratch=()):
    return pl.pallas_call(
        kernel,
        out_shape=outs,
        in_specs=specs,
        out_specs=jax.tree.map(lambda _: VMEM, outs),
        scratch_shapes=scratch,
        compiler_params=pltpu.CompilerParams(vmem_limit_bytes=40 * 1024 * 1024),
        cost_estimate=pl.CostEstimate(flops=flops, bytes_accessed=4_000_000, transcendentals=0),
    )


def embed(feats, head):
    raw = jnp.dot(feats, head, preferred_element_type=F32)
    inverse = lax.rsqrt(jnp.sum(raw * raw, axis=-1, keepdims=True) + EPSILON)
    return (raw * inverse, inverse)


def video_kernel(feats, head, whole, first, second):
    unit, unused_inv = embed(feats[...], head[...])
    emb = unit.astype(BF16)
    cut = first.shape[0]
    whole[...] = emb
    first[...] = emb[:cut]
    second[...] = emb[cut:]


def weighted(sharp, offset, emb, block, diagonal):
    scores = sharp * lax.dot_general(emb, block, NT, preferred_element_type=F32) + offset
    if diagonal:
        row = lax.broadcasted_iota(jnp.int32, scores.shape, 0)
        col = lax.broadcasted_iota(jnp.int32, scores.shape, 1)
        sign = jnp.where(row == col, 1.0, -1.0).astype(F32)
        weight = -sign * jax.nn.sigmoid(-sign * scores)
    else:
        weight = jax.nn.sigmoid(scores)
    return jnp.dot(weight.astype(BF16), block, preferred_element_type=F32)


def text_kernel(feats, head, unit, inv, emb):
    text_unit, text_inv = embed(feats[...], head[...])
    unit[...] = text_unit
    inv[...] = jnp.broadcast_to(text_inv, inv.shape)
    emb[...] = text_unit.astype(BF16)


def near_kernel(sharp, offset, place, emb, own, row, total):
    acc = weighted(sharp[0], offset[0], emb[...], own[...], True)
    for k in (1, 2, 3):
        acc += weighted(sharp[0], offset[0], emb[...], row[lax.rem(place[0] + k, 4)], False)
    total[...] = acc


def far_sum(sharp, offset, emb, total, b0, b1, b2, b3):
    acc = total[...]
    for pair in ((b0, b1), (b2, b3)):
        block = jnp.concatenate([pair[0][...], pair[1][...]], axis=0)
        acc += weighted(sharp[0], offset[0], emb[...], block, False)
    return acc


def far_kernel(sharp, offset, emb, total, b0, b1, b2, b3, out):
    out[...] = far_sum(sharp, offset, emb, total, b0, b1, b2, b3)


def last_kernel(sharp, offset, emb, total, b0, b1, b2, b3, unit, inv, theirs, out, packed):
    grad = sharp[0] * far_sum(sharp, offset, emb, total, b0, b1, b2, b3)
    text_unit = unit[...]
    inner = jnp.sum(text_unit * grad, axis=-1, keepdims=True)
    raw = (inv[:, :1] * (grad - text_unit * inner)).astype(BF16)
    out[...] = raw
    packed[:256] = raw
    for k in range(3):
        packed[256:, 256 * k : 256 * k + 256] = theirs[192 * k : 192 * k + 192]


def term_kernel(mine, raw, other, out, term):
    term[...] = jnp.dot(mine[...], raw[...], preferred_element_type=F32)
    for k in range(3):
        columns = other[256:, 256 * k : 256 * k + 256]
        term[192 * k : 192 * k + 192] += jnp.dot(columns, other[:256], preferred_element_type=F32)
    low = lax.broadcasted_iota(jnp.int32, (72, 128), 1) < 64
    pad = jnp.zeros((8, 128), F32)
    for y in range(4):
        rows = 144 * y
        for k in range(2):
            middle = 384 * k + 128
            a = term[rows : rows + 72, middle : middle + 128]
            b = term[rows + 72 : rows + 144, middle : middle + 128]
            even = jnp.where(low, a, pltpu.roll(b, 64, 1))
            odd = jnp.where(low, pltpu.roll(a, 64, 1), b)
            for x, main, rest in ((2 * k, 384 * k, even), (2 * k + 1, 384 * k + 256, odd)):
                out[4 * y + x, 0:144, :] = term[rows : rows + 144, main : main + 128].astype(BF16)
                out[4 * y + x, 144:224, :] = jnp.concatenate([rest, pad], axis=0).astype(BF16)


def local(
    visual_tower_outputs,
    language_tower_outputs,
    visual_mapping_frozen,
    language_mapping_learnable,
    sigmoid_sharpness_array,
    sigmoid_offset_array,
):
    rows, feat = language_tower_outputs.shape
    width = visual_mapping_frozen.shape[1]
    ny, nzl, nc, nx, nzh = SIZES
    devices = ny * nzl * nc * nx * nzh
    piece_r = feat // (ny * nzl * nc)
    piece_c = width // (nx * nzh)
    core = lax.axis_index("c")
    scalars = (sigmoid_sharpness_array, sigmoid_offset_array)
    part = rows // 2
    dots = 2 * rows * rows * width

    def shape(*dims, kind=BF16):
        return jax.ShapeDtypeStruct(dims, kind)

    whole, first, second = call(
        video_kernel,
        [shape(rows, width), shape(part, width), shape(part, width)],
        [VMEM] * 2,
        2 * rows * feat * width,
    )(visual_tower_outputs, visual_mapping_frozen)

    def around(block):
        return [lax.ppermute(block, "x", ring(nx, k)) for k in (2, 1, 3)]

    first = lax.ppermute(first, "zh", ring(2, 1))
    second = lax.ppermute(second, "zh", ring(2, 1))
    near = lax.all_gather(whole, "x")

    unit, inv, emb = call(
        text_kernel,
        [shape(rows, width, kind=F32), shape(rows, 128, kind=F32), shape(rows, width)],
        [VMEM] * 2,
        2 * rows * feat * width,
    )(language_tower_outputs, language_mapping_learnable)

    half = feat // 2
    place = lax.broadcasted_iota(jnp.int32, (half, feat), 0)
    source = lax.broadcasted_iota(jnp.int32, (half, feat), 1)
    start = (place // piece_r) * (2 * piece_r) + place % piece_r

    def columns_of(which):
        pick = (source == start + which * piece_r).astype(BF16)
        return lax.dot_general(
            pick, language_tower_outputs, NT, preferred_element_type=F32
        ).astype(BF16)

    mine = columns_of(core)
    theirs = columns_of(1 - core)

    first, mine, theirs, emb = lax.optimization_barrier((first, mine, theirs, emb))
    total = call(near_kernel, shape(rows, width, kind=F32), [SMEM] * 3 + [VMEM] * 3, 8 * dots)(
        *scalars, lax.axis_index("x").reshape(1), emb, whole, near
    )
    total = call(far_kernel, shape(rows, width, kind=F32), [SMEM] * 2 + [VMEM] * 6, 4 * dots)(
        *scalars, emb, total, first, *around(first)
    )
    raw_grad, packed = call(
        last_kernel,
        [shape(rows, width), shape(rows + half // 3, width)],
        [SMEM] * 2 + [VMEM] * 9,
        4 * dots,
    )(*scalars, emb, total, second, *around(second), unit, inv, theirs)

    other = lax.ppermute(packed, "c", ring(2, 1))
    text_grad = lax.dot_general(
        raw_grad, language_mapping_learnable, NT, preferred_element_type=F32
    ).astype(BF16)
    other, text_grad = lax.optimization_barrier((other, text_grad))

    term = call(
        term_kernel,
        shape(ny * nx, 224, 128),
        [VMEM] * 3,
        4 * half * rows * width,
        scratch=[pltpu.VMEM((half, width), F32)],
    )(mine, raw_grad, other)
    term = lax.all_to_all(term, ("y", "x"), 0, 0, tiled=True)
    term = jnp.sum(term.astype(F32), axis=0)
    main = term[:144]
    rest = jnp.concatenate([term[144:216, :64], term[144:216, 64:]], axis=0)
    is_even = lax.axis_index("x") % 2 == 0
    term = jnp.where(
        is_even, jnp.concatenate([main, rest], axis=1), jnp.concatenate([rest, main], axis=1)
    ).astype(BF16)
    term = term.reshape(nzl, piece_r, nzh, piece_c).transpose(0, 2, 1, 3)
    term = term.reshape(nzl * nzh, piece_r, piece_c)
    term = lax.all_to_all(term, ("zl", "zh"), 0, 0, tiled=True)
    head_grad = jnp.sum(term.astype(F32), axis=0) / F32(devices)
    return (text_grad, head_grad)


def solution(mesh):
    fine = Mesh(mesh.devices.reshape(SIZES), AXES)
    pairs = P(("y", "zl", "c", "x", "zh"), None)
    return jax.shard_map(
        local,
        mesh=fine,
        in_specs=(pairs, pairs, P(), P(), P(), P()),
        out_specs=(pairs, P(("y", "zl", "c"), ("x", "zh"))),
        check_vma=False,
    )
```

```python
import jax
import jax.numpy as jnp
from jax import lax
from jax.experimental import pallas as pl
from jax.experimental.pallas import tpu as pltpu
from jax.sharding import Mesh, PartitionSpec as P

EPSILON = 1e-06
AXES = ("y", "zl", "c", "x", "zh")
SIZES = (4, 8, 2, 4, 2)
F32 = jnp.float32
BF16 = jnp.bfloat16
VMEM = pl.BlockSpec(memory_space=pltpu.VMEM)
SMEM = pl.BlockSpec(memory_space=pltpu.SMEM)
NT = (((1,), (1,)), ((), ()))


def ring(n, step):
    return [(i, (i + step) % n) for i in range(n)]


def call(kernel, outs, specs, flops, scratch=()):
    return pl.pallas_call(
        kernel,
        out_shape=outs,
        in_specs=specs,
        out_specs=jax.tree.map(lambda _: VMEM, outs),
        scratch_shapes=scratch,
        compiler_params=pltpu.CompilerParams(vmem_limit_bytes=40 * 1024 * 1024),
        cost_estimate=pl.CostEstimate(flops=flops, bytes_accessed=4_000_000, transcendentals=0),
    )


def embed(feats, head):
    raw = jnp.dot(feats, head, preferred_element_type=F32)
    inverse = lax.rsqrt(jnp.sum(raw * raw, axis=-1, keepdims=True) + EPSILON)
    return (raw * inverse, inverse)


def video_kernel(feats, head, whole, first, second):
    unit, unused_inv = embed(feats[...], head[...])
    emb = unit.astype(BF16)
    cut = first.shape[0]
    whole[...] = emb
    first[...] = emb[:cut]
    second[...] = emb[cut:]


def weighted(sharp, offset, emb, block, diagonal):
    scores = sharp * lax.dot_general(emb, block, NT, preferred_element_type=F32) + offset
    if diagonal:
        row = lax.broadcasted_iota(jnp.int32, scores.shape, 0)
        col = lax.broadcasted_iota(jnp.int32, scores.shape, 1)
        sign = jnp.where(row == col, 1.0, -1.0).astype(F32)
        weight = -sign * jax.nn.sigmoid(-sign * scores)
    else:
        weight = jax.nn.sigmoid(scores)
    return jnp.dot(weight.astype(BF16), block, preferred_element_type=F32)


def text_kernel(feats, head, unit, inv, emb):
    text_unit, text_inv = embed(feats[...], head[...])
    unit[...] = text_unit
    inv[...] = jnp.broadcast_to(text_inv, inv.shape)
    emb[...] = text_unit.astype(BF16)


def near_kernel(sharp, offset, emb, b0, b1, b2, b3, total):
    acc = weighted(sharp[0], offset[0], emb[...], b0[...], True)
    for block in (b1, b2, b3):
        acc += weighted(sharp[0], offset[0], emb[...], block[...], False)
    total[...] = acc


def far_sum(sharp, offset, emb, total, b0, b1, b2, b3):
    acc = total[...]
    for pair in ((b0, b1), (b2, b3)):
        block = jnp.concatenate([pair[0][...], pair[1][...]], axis=0)
        acc += weighted(sharp[0], offset[0], emb[...], block, False)
    return acc


def far_kernel(sharp, offset, emb, total, b0, b1, b2, b3, out):
    out[...] = far_sum(sharp, offset, emb, total, b0, b1, b2, b3)


def last_kernel(sharp, offset, emb, total, b0, b1, b2, b3, unit, inv, theirs, out, packed):
    grad = sharp[0] * far_sum(sharp, offset, emb, total, b0, b1, b2, b3)
    text_unit = unit[...]
    inner = jnp.sum(text_unit * grad, axis=-1, keepdims=True)
    raw = (inv[:, :1] * (grad - text_unit * inner)).astype(BF16)
    out[...] = raw
    packed[:256] = raw
    for k in range(3):
        packed[256:, 256 * k : 256 * k + 256] = theirs[192 * k : 192 * k + 192]


def term_kernel(mine, raw, other, out, term):
    term[...] = jnp.dot(mine[...], raw[...], preferred_element_type=F32)
    for k in range(3):
        columns = other[256:, 256 * k : 256 * k + 256]
        term[192 * k : 192 * k + 192] += jnp.dot(columns, other[:256], preferred_element_type=F32)
    low = lax.broadcasted_iota(jnp.int32, (72, 128), 1) < 64
    pad = jnp.zeros((8, 128), F32)
    for y in range(4):
        rows = 144 * y
        for k in range(2):
            middle = 384 * k + 128
            a = term[rows : rows + 72, middle : middle + 128]
            b = term[rows + 72 : rows + 144, middle : middle + 128]
            even = jnp.where(low, a, pltpu.roll(b, 64, 1))
            odd = jnp.where(low, pltpu.roll(a, 64, 1), b)
            for x, main, rest in ((2 * k, 384 * k, even), (2 * k + 1, 384 * k + 256, odd)):
                out[4 * y + x, 0:144, :] = term[rows : rows + 144, main : main + 128].astype(BF16)
                out[4 * y + x, 144:224, :] = jnp.concatenate([rest, pad], axis=0).astype(BF16)


def local(
    visual_tower_outputs,
    language_tower_outputs,
    visual_mapping_frozen,
    language_mapping_learnable,
    sigmoid_sharpness_array,
    sigmoid_offset_array,
):
    rows, feat = language_tower_outputs.shape
    width = visual_mapping_frozen.shape[1]
    ny, nzl, nc, nx, nzh = SIZES
    devices = ny * nzl * nc * nx * nzh
    piece_r = feat // (ny * nzl * nc)
    piece_c = width // (nx * nzh)
    core = lax.axis_index("c")
    scalars = (sigmoid_sharpness_array, sigmoid_offset_array)
    part = rows // 2
    dots = 2 * rows * rows * width

    def shape(*dims, kind=BF16):
        return jax.ShapeDtypeStruct(dims, kind)

    whole, first, second = call(
        video_kernel,
        [shape(rows, width), shape(part, width), shape(part, width)],
        [VMEM] * 2,
        2 * rows * feat * width,
    )(visual_tower_outputs, visual_mapping_frozen)

    def around(block):
        return [lax.ppermute(block, "x", ring(nx, k)) for k in (2, 1, 3)]

    first = lax.ppermute(first, "zh", ring(2, 1))

    half = feat // 2
    place = lax.broadcasted_iota(jnp.int32, (half, feat), 0)
    source = lax.broadcasted_iota(jnp.int32, (half, feat), 1)
    start = (place // piece_r) * (2 * piece_r) + place % piece_r

    def columns_of(which):
        pick = (source == start + which * piece_r).astype(BF16)
        return lax.dot_general(
            pick, language_tower_outputs, NT, preferred_element_type=F32
        ).astype(BF16)

    mine = columns_of(core)
    theirs = columns_of(1 - core)
    whole, mine, theirs = lax.optimization_barrier((whole, mine, theirs))
    near = around(whole)

    second, first = lax.optimization_barrier((second, first))
    second = lax.ppermute(second, "zh", ring(2, 1))
    feats, first = lax.optimization_barrier((language_tower_outputs, first))
    unit, inv, emb = call(
        text_kernel,
        [shape(rows, width, kind=F32), shape(rows, 128, kind=F32), shape(rows, width)],
        [VMEM] * 2,
        20_000_000_000,
    )(feats, language_mapping_learnable)
    first, mine, theirs, emb, near = lax.optimization_barrier((first, mine, theirs, emb, near))
    total = call(near_kernel, shape(rows, width, kind=F32), [SMEM] * 2 + [VMEM] * 5, 8 * dots)(
        *scalars, emb, whole, *near
    )
    total = call(far_kernel, shape(rows, width, kind=F32), [SMEM] * 2 + [VMEM] * 6, 4 * dots)(
        *scalars, emb, total, first, *around(first)
    )
    raw_grad, packed = call(
        last_kernel,
        [shape(rows, width), shape(rows + half // 3, width)],
        [SMEM] * 2 + [VMEM] * 9,
        4 * dots,
    )(*scalars, emb, total, second, *around(second), unit, inv, theirs)

    other = lax.ppermute(packed, "c", ring(2, 1))
    text_grad = lax.dot_general(
        raw_grad, language_mapping_learnable, NT, preferred_element_type=F32
    ).astype(BF16)
    other, text_grad = lax.optimization_barrier((other, text_grad))

    term = call(
        term_kernel,
        shape(ny * nx, 224, 128),
        [VMEM] * 3,
        4 * half * rows * width,
        scratch=[pltpu.VMEM((half, width), F32)],
    )(mine, raw_grad, other)
    term = lax.all_to_all(term, ("y", "x"), 0, 0, tiled=True)
    term = jnp.sum(term.astype(F32), axis=0)
    main = term[:144]
    rest = jnp.concatenate([term[144:216, :64], term[144:216, 64:]], axis=0)
    is_even = lax.axis_index("x") % 2 == 0
    term = jnp.where(
        is_even, jnp.concatenate([main, rest], axis=1), jnp.concatenate([rest, main], axis=1)
    ).astype(BF16)
    term = term.reshape(nzl, piece_r, nzh, piece_c).transpose(0, 2, 1, 3)
    term = term.reshape(nzl * nzh, piece_r, piece_c)
    term = lax.all_to_all(term, ("zl", "zh"), 0, 0, tiled=True)
    head_grad = jnp.sum(term.astype(F32), axis=0) / F32(devices)
    return (text_grad, head_grad)


def solution(mesh):
    fine = Mesh(mesh.devices.reshape(SIZES), AXES)
    pairs = P(("y", "zl", "c", "x", "zh"), None)
    return jax.shard_map(
        local,
        mesh=fine,
        in_specs=(pairs, pairs, P(), P(), P(), P()),
        out_specs=(pairs, P(("y", "zl", "c"), ("x", "zh"))),
        check_vma=False,
    )
```

```python
import jax
import jax.numpy as jnp
from jax import lax
from jax.experimental import pallas as pl
from jax.experimental.pallas import tpu as pltpu
from jax.sharding import Mesh, PartitionSpec as P

EPSILON = 1e-06
AXES = ("y", "zl", "c", "x", "zh")
SIZES = (4, 8, 2, 4, 2)
F32 = jnp.float32
BF16 = jnp.bfloat16
VMEM = pl.BlockSpec(memory_space=pltpu.VMEM)
SMEM = pl.BlockSpec(memory_space=pltpu.SMEM)
NT = (((1,), (1,)), ((), ()))


def ring(n, step):
    return [(i, (i + step) % n) for i in range(n)]


def call(kernel, outs, specs, flops, scratch=()):
    return pl.pallas_call(
        kernel,
        out_shape=outs,
        in_specs=specs,
        out_specs=jax.tree.map(lambda _: VMEM, outs),
        scratch_shapes=scratch,
        compiler_params=pltpu.CompilerParams(vmem_limit_bytes=40 * 1024 * 1024),
        cost_estimate=pl.CostEstimate(flops=flops, bytes_accessed=4_000_000, transcendentals=0),
    )


def embed(feats, head):
    raw = jnp.dot(feats, head, preferred_element_type=F32)
    inverse = lax.rsqrt(jnp.sum(raw * raw, axis=-1, keepdims=True) + EPSILON)
    return (raw * inverse, inverse)


def video_kernel(feats, head, copies, first, second):
    unit, unused_inv = embed(feats[...], head[...])
    emb = unit.astype(BF16)
    cut = first.shape[0]
    for k in range(copies.shape[0]):
        copies[k] = emb
    first[...] = emb[:cut]
    second[...] = emb[cut:]


def weighted(sharp, offset, emb, block, diagonal):
    scores = sharp * lax.dot_general(emb, block, NT, preferred_element_type=F32) + offset
    if diagonal:
        row = lax.broadcasted_iota(jnp.int32, scores.shape, 0)
        col = lax.broadcasted_iota(jnp.int32, scores.shape, 1)
        sign = jnp.where(row == col, 1.0, -1.0).astype(F32)
        weight = -sign * jax.nn.sigmoid(-sign * scores)
    else:
        weight = jax.nn.sigmoid(scores)
    return jnp.dot(weight.astype(BF16), block, preferred_element_type=F32)


def text_kernel(feats, head, unit, inv, emb):
    text_unit, text_inv = embed(feats[...], head[...])
    unit[...] = text_unit
    inv[...] = jnp.broadcast_to(text_inv, inv.shape)
    emb[...] = text_unit.astype(BF16)


def near_kernel(sharp, offset, place, emb, row, total):
    acc = weighted(sharp[0], offset[0], emb[...], row[place[0]], True)
    for k in (1, 2, 3):
        acc += weighted(sharp[0], offset[0], emb[...], row[lax.rem(place[0] + k, 4)], False)
    total[...] = acc


def far_sum(sharp, offset, emb, total, b0, b1, b2, b3):
    acc = total[...]
    for pair in ((b0, b1), (b2, b3)):
        block = jnp.concatenate([pair[0][...], pair[1][...]], axis=0)
        acc += weighted(sharp[0], offset[0], emb[...], block, False)
    return acc


def far_kernel(sharp, offset, emb, total, b0, b1, b2, b3, out):
    out[...] = far_sum(sharp, offset, emb, total, b0, b1, b2, b3)


def last_kernel(sharp, offset, emb, total, b0, b1, b2, b3, unit, inv, theirs, out, packed):
    grad = sharp[0] * far_sum(sharp, offset, emb, total, b0, b1, b2, b3)
    text_unit = unit[...]
    inner = jnp.sum(text_unit * grad, axis=-1, keepdims=True)
    raw = (inv[:, :1] * (grad - text_unit * inner)).astype(BF16)
    out[...] = raw
    packed[:256] = raw
    for k in range(3):
        packed[256:, 256 * k : 256 * k + 256] = theirs[192 * k : 192 * k + 192]


def term_kernel(mine, raw, other, out, term):
    term[...] = jnp.dot(mine[...], raw[...], preferred_element_type=F32)
    for k in range(3):
        columns = other[256:, 256 * k : 256 * k + 256]
        term[192 * k : 192 * k + 192] += jnp.dot(columns, other[:256], preferred_element_type=F32)
    low = lax.broadcasted_iota(jnp.int32, (72, 128), 1) < 64
    pad = jnp.zeros((8, 128), F32)
    for y in range(4):
        rows = 144 * y
        for k in range(2):
            middle = 384 * k + 128
            a = term[rows : rows + 72, middle : middle + 128]
            b = term[rows + 72 : rows + 144, middle : middle + 128]
            even = jnp.where(low, a, pltpu.roll(b, 64, 1))
            odd = jnp.where(low, pltpu.roll(a, 64, 1), b)
            for x, main, rest in ((2 * k, 384 * k, even), (2 * k + 1, 384 * k + 256, odd)):
                out[4 * y + x, 0:144, :] = term[rows : rows + 144, main : main + 128].astype(BF16)
                out[4 * y + x, 144:224, :] = jnp.concatenate([rest, pad], axis=0).astype(BF16)


def local(
    visual_tower_outputs,
    language_tower_outputs,
    visual_mapping_frozen,
    language_mapping_learnable,
    sigmoid_sharpness_array,
    sigmoid_offset_array,
):
    rows, feat = language_tower_outputs.shape
    width = visual_mapping_frozen.shape[1]
    ny, nzl, nc, nx, nzh = SIZES
    devices = ny * nzl * nc * nx * nzh
    piece_r = feat // (ny * nzl * nc)
    piece_c = width // (nx * nzh)
    core = lax.axis_index("c")
    scalars = (sigmoid_sharpness_array, sigmoid_offset_array)
    part = rows // 2
    dots = 2 * rows * rows * width

    def shape(*dims, kind=BF16):
        return jax.ShapeDtypeStruct(dims, kind)

    copies, first, second = call(
        video_kernel,
        [shape(nx, rows, width), shape(part, width), shape(part, width)],
        [VMEM] * 2,
        2 * rows * feat * width,
    )(visual_tower_outputs, visual_mapping_frozen)

    def around(block):
        return [lax.ppermute(block, "x", ring(nx, k)) for k in (2, 1, 3)]

    first = lax.ppermute(first, "zh", ring(2, 1))

    second = lax.ppermute(second, "zh", ring(2, 1))
    near = lax.all_to_all(copies, "x", 0, 0, tiled=True)
    unit, inv, emb = call(
        text_kernel,
        [shape(rows, width, kind=F32), shape(rows, 128, kind=F32), shape(rows, width)],
        [VMEM] * 2,
        2 * rows * feat * width,
    )(language_tower_outputs, language_mapping_learnable)

    half = feat // 2
    place = lax.broadcasted_iota(jnp.int32, (half, feat), 0)
    source = lax.broadcasted_iota(jnp.int32, (half, feat), 1)
    start = (place // piece_r) * (2 * piece_r) + place % piece_r

    def columns_of(which):
        pick = (source == start + which * piece_r).astype(BF16)
        return lax.dot_general(
            pick, language_tower_outputs, NT, preferred_element_type=F32
        ).astype(BF16)

    mine = columns_of(core)
    theirs = columns_of(1 - core)

    place = lax.axis_index("x")
    is_even = place % 2 == 0
    first, mine, theirs, emb, near = lax.optimization_barrier((first, mine, theirs, emb, near))
    total = call(near_kernel, shape(rows, width, kind=F32), [SMEM] * 3 + [VMEM] * 2, 8 * dots)(
        *scalars, place.reshape(1), emb, near
    )
    total = call(far_kernel, shape(rows, width, kind=F32), [SMEM] * 2 + [VMEM] * 6, 4 * dots)(
        *scalars, emb, total, first, *around(first)
    )
    raw_grad, packed = call(
        last_kernel,
        [shape(rows, width), shape(rows + half // 3, width)],
        [SMEM] * 2 + [VMEM] * 9,
        4 * dots,
    )(*scalars, emb, total, second, *around(second), unit, inv, theirs)

    other = lax.ppermute(packed, "c", ring(2, 1))
    text_grad = lax.dot_general(
        raw_grad, language_mapping_learnable, NT, preferred_element_type=F32
    ).astype(BF16)
    other, text_grad, is_even = lax.optimization_barrier((other, text_grad, is_even))

    term = call(
        term_kernel,
        shape(ny * nx, 224, 128),
        [VMEM] * 3,
        4 * half * rows * width,
        scratch=[pltpu.VMEM((half, width), F32)],
    )(mine, raw_grad, other)
    term = lax.all_to_all(term, ("y", "x"), 0, 0, tiled=True)
    term = jnp.sum(term.astype(F32), axis=0)
    main = term[:144]
    rest = jnp.concatenate([term[144:216, :64], term[144:216, 64:]], axis=0)
    term = jnp.where(
        is_even, jnp.concatenate([main, rest], axis=1), jnp.concatenate([rest, main], axis=1)
    ).astype(BF16)
    term = term.reshape(nzl, piece_r, nzh, piece_c).transpose(0, 2, 1, 3)
    term = term.reshape(nzl * nzh, piece_r, piece_c)
    term = lax.all_to_all(term, ("zl", "zh"), 0, 0, tiled=True)
    head_grad = jnp.sum(term.astype(F32), axis=0) / F32(devices)
    return (text_grad, head_grad)


def solution(mesh):
    fine = Mesh(mesh.devices.reshape(SIZES), AXES)
    pairs = P(("y", "zl", "c", "x", "zh"), None)
    return jax.shard_map(
        local,
        mesh=fine,
        in_specs=(pairs, pairs, P(), P(), P(), P()),
        out_specs=(pairs, P(("y", "zl", "c"), ("x", "zh"))),
        check_vma=False,
    )
```

```python
import jax
import jax.numpy as jnp
from jax import lax
from jax.experimental import pallas as pl
from jax.experimental.pallas import tpu as pltpu
from jax.sharding import Mesh, PartitionSpec as P

EPSILON = 1e-06
AXES = ("y", "zl", "c", "x", "zh")
SIZES = (4, 8, 2, 4, 2)
F32 = jnp.float32
BF16 = jnp.bfloat16
VMEM = pl.BlockSpec(memory_space=pltpu.VMEM)
SMEM = pl.BlockSpec(memory_space=pltpu.SMEM)
NT = (((1,), (1,)), ((), ()))


def ring(n, step):
    return [(i, (i + step) % n) for i in range(n)]


def call(kernel, outs, specs, flops, scratch=()):
    return pl.pallas_call(
        kernel,
        out_shape=outs,
        in_specs=specs,
        out_specs=jax.tree.map(lambda _: VMEM, outs),
        scratch_shapes=scratch,
        compiler_params=pltpu.CompilerParams(vmem_limit_bytes=40 * 1024 * 1024),
        cost_estimate=pl.CostEstimate(flops=flops, bytes_accessed=4_000_000, transcendentals=0),
    )


def embed(feats, head):
    raw = jnp.dot(feats, head, preferred_element_type=F32)
    inverse = lax.rsqrt(jnp.sum(raw * raw, axis=-1, keepdims=True) + EPSILON)
    return (raw * inverse, inverse)


def video_kernel(feats, head, whole):
    unit, unused_inv = embed(feats[...], head[...])
    whole[...] = unit.astype(BF16)


def copies_kernel(block, out):
    for k in range(out.shape[0]):
        out[k] = block[...]


def weighted(sharp, offset, emb, block, diagonal):
    scores = sharp * lax.dot_general(emb, block, NT, preferred_element_type=F32) + offset
    if diagonal:
        row = lax.broadcasted_iota(jnp.int32, scores.shape, 0)
        col = lax.broadcasted_iota(jnp.int32, scores.shape, 1)
        sign = jnp.where(row == col, 1.0, -1.0).astype(F32)
        weight = -sign * jax.nn.sigmoid(-sign * scores)
    else:
        weight = jax.nn.sigmoid(scores)
    return jnp.dot(weight.astype(BF16), block, preferred_element_type=F32)


def text_kernel(feats, head, unit, inv, emb):
    text_unit, text_inv = embed(feats[...], head[...])
    unit[...] = text_unit
    inv[...] = jnp.broadcast_to(text_inv, inv.shape)
    emb[...] = text_unit.astype(BF16)


def near_kernel(sharp, offset, emb, b0, b1, b2, b3, total):
    acc = weighted(sharp[0], offset[0], emb[...], b0[...], True)
    for block in (b1, b2, b3):
        acc += weighted(sharp[0], offset[0], emb[...], block[...], False)
    total[...] = acc


def last_kernel(sharp, offset, emb, total, row, unit, inv, theirs, out, packed):
    acc = total[...]
    for k in range(row.shape[0]):
        acc += weighted(sharp[0], offset[0], emb[...], row[k], False)
    grad = sharp[0] * acc
    text_unit = unit[...]
    inner = jnp.sum(text_unit * grad, axis=-1, keepdims=True)
    raw = (inv[:, :1] * (grad - text_unit * inner)).astype(BF16)
    out[...] = raw
    packed[:256] = raw
    for k in range(3):
        packed[256:, 256 * k : 256 * k + 256] = theirs[192 * k : 192 * k + 192]


def term_kernel(mine, raw, other, out, term):
    term[...] = jnp.dot(mine[...], raw[...], preferred_element_type=F32)
    for k in range(3):
        columns = other[256:, 256 * k : 256 * k + 256]
        term[192 * k : 192 * k + 192] += jnp.dot(columns, other[:256], preferred_element_type=F32)
    low = lax.broadcasted_iota(jnp.int32, (72, 128), 1) < 64
    pad = jnp.zeros((8, 128), F32)
    for y in range(4):
        rows = 144 * y
        for k in range(2):
            middle = 384 * k + 128
            a = term[rows : rows + 72, middle : middle + 128]
            b = term[rows + 72 : rows + 144, middle : middle + 128]
            even = jnp.where(low, a, pltpu.roll(b, 64, 1))
            odd = jnp.where(low, pltpu.roll(a, 64, 1), b)
            for x, main, rest in ((2 * k, 384 * k, even), (2 * k + 1, 384 * k + 256, odd)):
                out[4 * y + x, 0:144, :] = term[rows : rows + 144, main : main + 128].astype(BF16)
                out[4 * y + x, 144:224, :] = jnp.concatenate([rest, pad], axis=0).astype(BF16)


def local(
    visual_tower_outputs,
    language_tower_outputs,
    visual_mapping_frozen,
    language_mapping_learnable,
    sigmoid_sharpness_array,
    sigmoid_offset_array,
):
    rows, feat = language_tower_outputs.shape
    width = visual_mapping_frozen.shape[1]
    ny, nzl, nc, nx, nzh = SIZES
    devices = ny * nzl * nc * nx * nzh
    piece_r = feat // (ny * nzl * nc)
    piece_c = width // (nx * nzh)
    core = lax.axis_index("c")
    scalars = (sigmoid_sharpness_array, sigmoid_offset_array)
    dots = 2 * rows * rows * width

    def shape(*dims, kind=BF16):
        return jax.ShapeDtypeStruct(dims, kind)

    whole = call(
        video_kernel,
        shape(rows, width),
        [VMEM] * 2,
        2 * rows * feat * width,
    )(visual_tower_outputs, visual_mapping_frozen)

    def around(block):
        return [lax.ppermute(block, "x", ring(nx, k)) for k in (2, 1, 3)]

    across = lax.ppermute(whole, "zh", ring(2, 1))

    half = feat // 2
    place = lax.broadcasted_iota(jnp.int32, (half, feat), 0)
    source = lax.broadcasted_iota(jnp.int32, (half, feat), 1)
    start = (place // piece_r) * (2 * piece_r) + place % piece_r

    def columns_of(which):
        pick = (source == start + which * piece_r).astype(BF16)
        return lax.dot_general(
            pick, language_tower_outputs, NT, preferred_element_type=F32
        ).astype(BF16)

    mine = columns_of(core)
    theirs = columns_of(1 - core)
    whole, mine, theirs = lax.optimization_barrier((whole, mine, theirs))
    near = around(whole)

    unit, inv, emb = call(
        text_kernel,
        [shape(rows, width, kind=F32), shape(rows, 128, kind=F32), shape(rows, width)],
        [VMEM] * 2,
        2 * rows * feat * width,
    )(language_tower_outputs, language_mapping_learnable)
    total = call(near_kernel, shape(rows, width, kind=F32), [SMEM] * 2 + [VMEM] * 5, 8 * dots)(
        *scalars, emb, whole, *near
    )
    copies = call(copies_kernel, shape(nx, rows, width), [VMEM], 1_000_000)(across)
    far = lax.all_to_all(copies, "x", 0, 0, tiled=True)
    raw_grad, packed = call(
        last_kernel,
        [shape(rows, width), shape(rows + half // 3, width)],
        [SMEM] * 2 + [VMEM] * 6,
        8 * dots,
    )(*scalars, emb, total, far, unit, inv, theirs)

    other = lax.ppermute(packed, "c", ring(2, 1))
    text_grad = lax.dot_general(
        raw_grad, language_mapping_learnable, NT, preferred_element_type=F32
    ).astype(BF16)
    other, text_grad = lax.optimization_barrier((other, text_grad))

    term = call(
        term_kernel,
        shape(ny * nx, 224, 128),
        [VMEM] * 3,
        4 * half * rows * width,
        scratch=[pltpu.VMEM((half, width), F32)],
    )(mine, raw_grad, other)
    term = lax.all_to_all(term, ("y", "x"), 0, 0, tiled=True)
    term = jnp.sum(term.astype(F32), axis=0)
    main = term[:144]
    rest = jnp.concatenate([term[144:216, :64], term[144:216, 64:]], axis=0)
    is_even = lax.axis_index("x") % 2 == 0
    term = jnp.where(
        is_even, jnp.concatenate([main, rest], axis=1), jnp.concatenate([rest, main], axis=1)
    ).astype(BF16)
    term = term.reshape(nzl, piece_r, nzh, piece_c).transpose(0, 2, 1, 3)
    term = term.reshape(nzl * nzh, piece_r, piece_c)
    term = lax.all_to_all(term, ("zl", "zh"), 0, 0, tiled=True)
    head_grad = jnp.sum(term.astype(F32), axis=0) / F32(devices)
    return (text_grad, head_grad)


def solution(mesh):
    fine = Mesh(mesh.devices.reshape(SIZES), AXES)
    pairs = P(("y", "zl", "c", "x", "zh"), None)
    return jax.shard_map(
        local,
        mesh=fine,
        in_specs=(pairs, pairs, P(), P(), P(), P()),
        out_specs=(pairs, P(("y", "zl", "c"), ("x", "zh"))),
        check_vma=False,
    )
```

```python
import jax
import jax.numpy as jnp
from jax import lax
from jax.experimental import pallas as pl
from jax.experimental.pallas import tpu as pltpu
from jax.sharding import Mesh, PartitionSpec as P

EPSILON = 1e-06
AXES = ("y", "zl", "c", "x", "zh")
SIZES = (4, 8, 2, 4, 2)
F32 = jnp.float32
BF16 = jnp.bfloat16
VMEM = pl.BlockSpec(memory_space=pltpu.VMEM)
SMEM = pl.BlockSpec(memory_space=pltpu.SMEM)
NT = (((1,), (1,)), ((), ()))


def ring(n, step):
    return [(i, (i + step) % n) for i in range(n)]


def call(kernel, outs, specs, flops, scratch=()):
    return pl.pallas_call(
        kernel,
        out_shape=outs,
        in_specs=specs,
        out_specs=jax.tree.map(lambda _: VMEM, outs),
        scratch_shapes=scratch,
        compiler_params=pltpu.CompilerParams(vmem_limit_bytes=40 * 1024 * 1024),
        cost_estimate=pl.CostEstimate(flops=flops, bytes_accessed=4_000_000, transcendentals=0),
    )


def embed(feats, head):
    raw = jnp.dot(feats, head, preferred_element_type=F32)
    inverse = lax.rsqrt(jnp.sum(raw * raw, axis=-1, keepdims=True) + EPSILON)
    return (raw * inverse, inverse)


def video_kernel(feats, head, whole, first, second):
    unit, unused_inv = embed(feats[...], head[...])
    emb = unit.astype(BF16)
    cut = first.shape[0]
    whole[...] = emb
    first[...] = emb[:cut]
    for k in range(second.shape[0]):
        second[k] = emb[cut:]


def weighted(sharp, offset, emb, block, diagonal):
    scores = sharp * lax.dot_general(emb, block, NT, preferred_element_type=F32) + offset
    if diagonal:
        row = lax.broadcasted_iota(jnp.int32, scores.shape, 0)
        col = lax.broadcasted_iota(jnp.int32, scores.shape, 1)
        sign = jnp.where(row == col, 1.0, -1.0).astype(F32)
        weight = -sign * jax.nn.sigmoid(-sign * scores)
    else:
        weight = jax.nn.sigmoid(scores)
    return jnp.dot(weight.astype(BF16), block, preferred_element_type=F32)


def text_kernel(feats, head, unit, inv, emb):
    text_unit, text_inv = embed(feats[...], head[...])
    unit[...] = text_unit
    inv[...] = jnp.broadcast_to(text_inv, inv.shape)
    emb[...] = text_unit.astype(BF16)


def near_kernel(sharp, offset, emb, b0, b1, b2, b3, total):
    acc = weighted(sharp[0], offset[0], emb[...], b0[...], True)
    for block in (b1, b2, b3):
        acc += weighted(sharp[0], offset[0], emb[...], block[...], False)
    total[...] = acc


def far_sum(sharp, offset, emb, total, b0, b1, b2, b3):
    acc = total[...]
    for pair in ((b0, b1), (b2, b3)):
        block = jnp.concatenate([pair[0][...], pair[1][...]], axis=0)
        acc += weighted(sharp[0], offset[0], emb[...], block, False)
    return acc


def far_kernel(sharp, offset, emb, total, b0, b1, b2, b3, out):
    out[...] = far_sum(sharp, offset, emb, total, b0, b1, b2, b3)


def last_kernel(sharp, offset, emb, total, b0, b1, b2, b3, unit, inv, theirs, out, packed):
    grad = sharp[0] * far_sum(sharp, offset, emb, total, b0, b1, b2, b3)
    text_unit = unit[...]
    inner = jnp.sum(text_unit * grad, axis=-1, keepdims=True)
    raw = (inv[:, :1] * (grad - text_unit * inner)).astype(BF16)
    out[...] = raw
    packed[:256] = raw
    for k in range(3):
        packed[256:, 256 * k : 256 * k + 256] = theirs[192 * k : 192 * k + 192]


def term_kernel(mine, raw, other, out, term):
    term[...] = jnp.dot(mine[...], raw[...], preferred_element_type=F32)
    for k in range(3):
        columns = other[256:, 256 * k : 256 * k + 256]
        term[192 * k : 192 * k + 192] += jnp.dot(columns, other[:256], preferred_element_type=F32)
    low = lax.broadcasted_iota(jnp.int32, (72, 128), 1) < 64
    pad = jnp.zeros((8, 128), F32)
    for y in range(4):
        rows = 144 * y
        for k in range(2):
            middle = 384 * k + 128
            a = term[rows : rows + 72, middle : middle + 128]
            b = term[rows + 72 : rows + 144, middle : middle + 128]
            even = jnp.where(low, a, pltpu.roll(b, 64, 1))
            odd = jnp.where(low, pltpu.roll(a, 64, 1), b)
            for x, main, rest in ((2 * k, 384 * k, even), (2 * k + 1, 384 * k + 256, odd)):
                out[4 * y + x, 0:144, :] = term[rows : rows + 144, main : main + 128].astype(BF16)
                out[4 * y + x, 144:224, :] = jnp.concatenate([rest, pad], axis=0).astype(BF16)


def local(
    visual_tower_outputs,
    language_tower_outputs,
    visual_mapping_frozen,
    language_mapping_learnable,
    sigmoid_sharpness_array,
    sigmoid_offset_array,
):
    rows, feat = language_tower_outputs.shape
    width = visual_mapping_frozen.shape[1]
    ny, nzl, nc, nx, nzh = SIZES
    devices = ny * nzl * nc * nx * nzh
    piece_r = feat // (ny * nzl * nc)
    piece_c = width // (nx * nzh)
    core = lax.axis_index("c")
    scalars = (sigmoid_sharpness_array, sigmoid_offset_array)
    part = rows // 2
    dots = 2 * rows * rows * width

    def shape(*dims, kind=BF16):
        return jax.ShapeDtypeStruct(dims, kind)

    whole, first, second = call(
        video_kernel,
        [shape(rows, width), shape(part, width), shape(nzh, part, width)],
        [VMEM] * 2,
        2 * rows * feat * width,
    )(visual_tower_outputs, visual_mapping_frozen)

    def around(block):
        return [lax.ppermute(block, "x", ring(nx, k)) for k in (2, 1, 3)]

    first = lax.ppermute(first, "zh", ring(2, 1))
    second = lax.all_to_all(second, "zh", 0, 0, tiled=True)
    second = lax.dynamic_index_in_dim(second, 1 - lax.axis_index("zh"), 0, keepdims=False)

    half = feat // 2
    place = lax.broadcasted_iota(jnp.int32, (half, feat), 0)
    source = lax.broadcasted_iota(jnp.int32, (half, feat), 1)
    start = (place // piece_r) * (2 * piece_r) + place % piece_r

    def columns_of(which):
        pick = (source == start + which * piece_r).astype(BF16)
        return lax.dot_general(
            pick, language_tower_outputs, NT, preferred_element_type=F32
        ).astype(BF16)

    mine = columns_of(core)
    theirs = columns_of(1 - core)
    whole, mine, theirs = lax.optimization_barrier((whole, mine, theirs))
    near = around(whole)

    feats, first = lax.optimization_barrier((language_tower_outputs, first))
    unit, inv, emb = call(
        text_kernel,
        [shape(rows, width, kind=F32), shape(rows, 128, kind=F32), shape(rows, width)],
        [VMEM] * 2,
        20_000_000_000,
    )(feats, language_mapping_learnable)
    first, mine, theirs, emb, near = lax.optimization_barrier((first, mine, theirs, emb, near))
    total = call(near_kernel, shape(rows, width, kind=F32), [SMEM] * 2 + [VMEM] * 5, 8 * dots)(
        *scalars, emb, whole, *near
    )
    total = call(far_kernel, shape(rows, width, kind=F32), [SMEM] * 2 + [VMEM] * 6, 4 * dots)(
        *scalars, emb, total, first, *around(first)
    )
    raw_grad, packed = call(
        last_kernel,
        [shape(rows, width), shape(rows + half // 3, width)],
        [SMEM] * 2 + [VMEM] * 9,
        4 * dots,
    )(*scalars, emb, total, second, *around(second), unit, inv, theirs)

    other = lax.ppermute(packed, "c", ring(2, 1))
    text_grad = lax.dot_general(
        raw_grad, language_mapping_learnable, NT, preferred_element_type=F32
    ).astype(BF16)
    other, text_grad = lax.optimization_barrier((other, text_grad))

    term = call(
        term_kernel,
        shape(ny * nx, 224, 128),
        [VMEM] * 3,
        4 * half * rows * width,
        scratch=[pltpu.VMEM((half, width), F32)],
    )(mine, raw_grad, other)
    term = lax.all_to_all(term, ("y", "x"), 0, 0, tiled=True)
    term = jnp.sum(term.astype(F32), axis=0)
    main = term[:144]
    rest = jnp.concatenate([term[144:216, :64], term[144:216, 64:]], axis=0)
    is_even = lax.axis_index("x") % 2 == 0
    term = jnp.where(
        is_even, jnp.concatenate([main, rest], axis=1), jnp.concatenate([rest, main], axis=1)
    ).astype(BF16)
    term = term.reshape(nzl, piece_r, nzh, piece_c).transpose(0, 2, 1, 3)
    term = term.reshape(nzl * nzh, piece_r, piece_c)
    term = lax.all_to_all(term, ("zl", "zh"), 0, 0, tiled=True)
    head_grad = jnp.sum(term.astype(F32), axis=0) / F32(devices)
    return (text_grad, head_grad)


def solution(mesh):
    fine = Mesh(mesh.devices.reshape(SIZES), AXES)
    pairs = P(("y", "zl", "c", "x", "zh"), None)
    return jax.shard_map(
        local,
        mesh=fine,
        in_specs=(pairs, pairs, P(), P(), P(), P()),
        out_specs=(pairs, P(("y", "zl", "c"), ("x", "zh"))),
        check_vma=False,
    )
```

```python
import jax
import jax.numpy as jnp
from jax import lax
from jax.experimental import pallas as pl
from jax.experimental.pallas import tpu as pltpu
from jax.sharding import Mesh, PartitionSpec as P

EPSILON = 1e-06
AXES = ("y", "zl", "c", "x", "zh")
SIZES = (4, 8, 2, 4, 2)
F32 = jnp.float32
BF16 = jnp.bfloat16
VMEM = pl.BlockSpec(memory_space=pltpu.VMEM)
SMEM = pl.BlockSpec(memory_space=pltpu.SMEM)
NT = (((1,), (1,)), ((), ()))


def ring(n, step):
    return [(i, (i + step) % n) for i in range(n)]


def call(kernel, outs, specs, flops, scratch=()):
    return pl.pallas_call(
        kernel,
        out_shape=outs,
        in_specs=specs,
        out_specs=jax.tree.map(lambda _: VMEM, outs),
        scratch_shapes=scratch,
        compiler_params=pltpu.CompilerParams(vmem_limit_bytes=40 * 1024 * 1024),
        cost_estimate=pl.CostEstimate(flops=flops, bytes_accessed=4_000_000, transcendentals=0),
    )


def embed(feats, head):
    raw = jnp.dot(feats, head, preferred_element_type=F32)
    inverse = lax.rsqrt(jnp.sum(raw * raw, axis=-1, keepdims=True) + EPSILON)
    return (raw * inverse, inverse)


def video_kernel(feats, head, whole, first, second):
    unit, unused_inv = embed(feats[...], head[...])
    emb = unit.astype(BF16)
    cut = first.shape[0]
    whole[...] = emb
    first[...] = emb[:cut]
    second[...] = emb[cut:]


def weighted(sharp, offset, emb, block, diagonal):
    scores = sharp * lax.dot_general(emb, block, NT, preferred_element_type=F32) + offset
    if diagonal:
        row = lax.broadcasted_iota(jnp.int32, scores.shape, 0)
        col = lax.broadcasted_iota(jnp.int32, scores.shape, 1)
        sign = jnp.where(row == col, 1.0, -1.0).astype(F32)
        weight = -sign * jax.nn.sigmoid(-sign * scores)
    else:
        weight = jax.nn.sigmoid(scores)
    return jnp.dot(weight.astype(BF16), block, preferred_element_type=F32)


def text_kernel(feats, head, unit, inv, emb):
    text_unit, text_inv = embed(feats[...], head[...])
    unit[...] = text_unit
    inv[...] = jnp.broadcast_to(text_inv, inv.shape)
    emb[...] = text_unit.astype(BF16)


def near_kernel(sharp, offset, emb, b0, b1, b2, b3, total):
    acc = weighted(sharp[0], offset[0], emb[...], b0[...], True)
    for block in (b1, b2, b3):
        acc += weighted(sharp[0], offset[0], emb[...], block[...], False)
    total[...] = acc


def far_sum(sharp, offset, emb, total, b0, b1, b2, b3):
    acc = total[...]
    for pair in ((b0, b1), (b2, b3)):
        block = jnp.concatenate([pair[0][...], pair[1][...]], axis=0)
        acc += weighted(sharp[0], offset[0], emb[...], block, False)
    return acc


def far_kernel(sharp, offset, emb, total, b0, b1, b2, b3, out):
    out[...] = far_sum(sharp, offset, emb, total, b0, b1, b2, b3)


def last_kernel(sharp, offset, emb, total, b0, b1, b2, b3, unit, inv, theirs, out, packed):
    grad = sharp[0] * far_sum(sharp, offset, emb, total, b0, b1, b2, b3)
    text_unit = unit[...]
    inner = jnp.sum(text_unit * grad, axis=-1, keepdims=True)
    raw = (inv[:, :1] * (grad - text_unit * inner)).astype(BF16)
    out[...] = raw
    packed[:256] = raw
    for k in range(3):
        packed[256:, 256 * k : 256 * k + 256] = theirs[192 * k : 192 * k + 192]


def term_kernel(mine, raw, other, out, term):
    term[...] = jnp.dot(mine[...], raw[...], preferred_element_type=F32)
    for k in range(3):
        columns = other[256:, 256 * k : 256 * k + 256]
        term[192 * k : 192 * k + 192] += jnp.dot(columns, other[:256], preferred_element_type=F32)
    low = lax.broadcasted_iota(jnp.int32, (72, 128), 1) < 64
    pad = jnp.zeros((8, 128), F32)
    for y in range(4):
        rows = 144 * y
        for k in range(2):
            middle = 384 * k + 128
            a = term[rows : rows + 72, middle : middle + 128]
            b = term[rows + 72 : rows + 144, middle : middle + 128]
            even = jnp.where(low, a, pltpu.roll(b, 64, 1))
            odd = jnp.where(low, pltpu.roll(a, 64, 1), b)
            for x, main, rest in ((2 * k, 384 * k, even), (2 * k + 1, 384 * k + 256, odd)):
                out[4 * y + x, 0:144, :] = term[rows : rows + 144, main : main + 128].astype(BF16)
                out[4 * y + x, 144:224, :] = jnp.concatenate([rest, pad], axis=0).astype(BF16)


def local(
    visual_tower_outputs,
    language_tower_outputs,
    visual_mapping_frozen,
    language_mapping_learnable,
    sigmoid_sharpness_array,
    sigmoid_offset_array,
):
    rows, feat = language_tower_outputs.shape
    width = visual_mapping_frozen.shape[1]
    ny, nzl, nc, nx, nzh = SIZES
    devices = ny * nzl * nc * nx * nzh
    piece_r = feat // (ny * nzl * nc)
    piece_c = width // (nx * nzh)
    core = lax.axis_index("c")
    scalars = (sigmoid_sharpness_array, sigmoid_offset_array)
    part = rows // 2
    dots = 2 * rows * rows * width

    def shape(*dims, kind=BF16):
        return jax.ShapeDtypeStruct(dims, kind)

    whole, first, second = call(
        video_kernel,
        [shape(rows, width), shape(part, width), shape(part, width)],
        [VMEM] * 2,
        2 * rows * feat * width,
    )(visual_tower_outputs, visual_mapping_frozen)

    def around(block):
        return [lax.ppermute(block, "x", ring(nx, k)) for k in (2, 1, 3)]

    first = lax.ppermute(first, "zh", ring(2, 1))

    half = feat // 2
    place = lax.broadcasted_iota(jnp.int32, (half, feat), 0)
    source = lax.broadcasted_iota(jnp.int32, (half, feat), 1)
    start = (place // piece_r) * (2 * piece_r) + place % piece_r

    def columns_of(which):
        pick = (source == start + which * piece_r).astype(BF16)
        return lax.dot_general(
            pick, language_tower_outputs, NT, preferred_element_type=F32
        ).astype(BF16)

    mine = columns_of(core)
    theirs = columns_of(1 - core)
    whole, mine, theirs = lax.optimization_barrier((whole, mine, theirs))
    near = around(whole)

    second = lax.ppermute(second, "zh", ring(2, 1))
    feats, first = lax.optimization_barrier((language_tower_outputs, first))
    unit, inv, emb = call(
        text_kernel,
        [shape(rows, width, kind=F32), shape(rows, 128, kind=F32), shape(rows, width)],
        [VMEM] * 2,
        20_000_000_000,
    )(feats, language_mapping_learnable)
    first, mine, theirs, emb, near = lax.optimization_barrier((first, mine, theirs, emb, near))
    total = call(near_kernel, shape(rows, width, kind=F32), [SMEM] * 2 + [VMEM] * 5, 8 * dots)(
        *scalars, emb, whole, *near
    )
    total = call(far_kernel, shape(rows, width, kind=F32), [SMEM] * 2 + [VMEM] * 6, 4 * dots)(
        *scalars, emb, total, first, *around(first)
    )
    raw_grad, packed = call(
        last_kernel,
        [shape(rows, width), shape(rows + half // 3, width)],
        [SMEM] * 2 + [VMEM] * 9,
        4 * dots,
    )(*scalars, emb, total, second, *around(second), unit, inv, theirs)

    other = lax.ppermute(packed, "c", ring(2, 1))
    text_grad = lax.dot_general(
        raw_grad, language_mapping_learnable, NT, preferred_element_type=F32
    ).astype(BF16)
    other, text_grad = lax.optimization_barrier((other, text_grad))

    term = call(
        term_kernel,
        shape(ny * nx, 224, 128),
        [VMEM] * 3,
        4 * half * rows * width,
        scratch=[pltpu.VMEM((half, width), F32)],
    )(mine, raw_grad, other)
    term = lax.all_to_all(term, ("y", "x"), 0, 0, tiled=True)
    term = jnp.sum(term.astype(F32), axis=0)
    main = term[:144]
    rest = jnp.concatenate([term[144:216, :64], term[144:216, 64:]], axis=0)
    is_even = lax.axis_index("x") % 2 == 0
    term = jnp.where(
        is_even, jnp.concatenate([main, rest], axis=1), jnp.concatenate([rest, main], axis=1)
    ).astype(BF16)
    term = term.reshape(nzl, piece_r, nzh, piece_c).transpose(0, 2, 1, 3)
    term = term.reshape(nzl * nzh, piece_r, piece_c)
    term = lax.all_to_all(term, ("zl", "zh"), 0, 0, tiled=True)
    head_grad = jnp.sum(term.astype(F32), axis=0) / F32(devices)
    return (text_grad, head_grad)


def solution(mesh):
    fine = Mesh(mesh.devices.reshape(SIZES), AXES)
    pairs = P(("y", "zl", "c", "x", "zh"), None)
    return jax.shard_map(
        local,
        mesh=fine,
        in_specs=(pairs, pairs, P(), P(), P(), P()),
        out_specs=(pairs, P(("y", "zl", "c"), ("x", "zh"))),
        check_vma=False,
    )
```

```python
import jax
import jax.numpy as jnp
from jax import lax
from jax.experimental import pallas as pl
from jax.experimental.pallas import tpu as pltpu
from jax.sharding import Mesh, PartitionSpec as P

EPSILON = 1e-06
AXES = ("y", "zl", "c", "x", "zh")
SIZES = (4, 8, 2, 4, 2)
F32 = jnp.float32
BF16 = jnp.bfloat16
VMEM = pl.BlockSpec(memory_space=pltpu.VMEM)
SMEM = pl.BlockSpec(memory_space=pltpu.SMEM)
NT = (((1,), (1,)), ((), ()))


def ring(n, step):
    return [(i, (i + step) % n) for i in range(n)]


def call(kernel, outs, specs, flops, scratch=(), room=40):
    return pl.pallas_call(
        kernel,
        out_shape=outs,
        in_specs=specs,
        out_specs=jax.tree.map(lambda _: VMEM, outs),
        scratch_shapes=scratch,
        compiler_params=pltpu.CompilerParams(vmem_limit_bytes=room * 1024 * 1024),
        cost_estimate=pl.CostEstimate(flops=flops, bytes_accessed=4_000_000, transcendentals=0),
    )


def embed(feats, head):
    raw = jnp.dot(feats, head, preferred_element_type=F32)
    inverse = lax.rsqrt(jnp.sum(raw * raw, axis=-1, keepdims=True) + EPSILON)
    return (raw * inverse, inverse)


def video_kernel(feats, head, whole, first, second, feats_in, head_in, landed):
    pieces, depth = 6, feats.shape[1] // 3
    step = feats.shape[1] // pieces
    moves = []
    for k in range(pieces):
        rows = pl.ds(step * k, step)
        moves.append(pltpu.make_async_copy(head.at[rows], head_in.at[rows], landed.at[k]))
        if k % 2 == 0:
            lanes = pl.ds(depth * (k // 2), depth)
            moves.append(
                pltpu.make_async_copy(
                    feats.at[:, lanes], feats_in.at[:, lanes], landed.at[pieces + k // 2]
                )
            )
    for move in moves:
        move.start()
    raw = jnp.zeros(whole.shape, F32)
    for k in range(3):
        for move in moves[3 * k : 3 * k + 3]:
            move.wait()
        span = slice(depth * k, depth * k + depth)
        raw += jnp.dot(feats_in[:, span], head_in[span], preferred_element_type=F32)
    inverse = lax.rsqrt(jnp.sum(raw * raw, axis=-1, keepdims=True) + EPSILON)
    emb = (raw * inverse).astype(BF16)
    cut = first.shape[0]
    whole[...] = emb
    first[...] = emb[:cut]
    second[...] = emb[cut:]


def weighted(sharp, offset, emb, block, diagonal):
    scores = sharp * lax.dot_general(emb, block, NT, preferred_element_type=F32) + offset
    if diagonal:
        row = lax.broadcasted_iota(jnp.int32, scores.shape, 0)
        col = lax.broadcasted_iota(jnp.int32, scores.shape, 1)
        sign = jnp.where(row == col, 1.0, -1.0).astype(F32)
        weight = -sign * jax.nn.sigmoid(-sign * scores)
    else:
        weight = jax.nn.sigmoid(scores)
    return jnp.dot(weight.astype(BF16), block, preferred_element_type=F32)


def text_kernel(feats, head, unit, inv, emb):
    text_unit, text_inv = embed(feats[...], head[...])
    unit[...] = text_unit
    inv[...] = jnp.broadcast_to(text_inv, inv.shape)
    emb[...] = text_unit.astype(BF16)


def near_kernel(sharp, offset, emb, b0, b1, b2, b3, total):
    acc = weighted(sharp[0], offset[0], emb[...], b0[...], True)
    for block in (b1, b2, b3):
        acc += weighted(sharp[0], offset[0], emb[...], block[...], False)
    total[...] = acc


def far_sum(sharp, offset, emb, total, b0, b1, b2, b3):
    acc = total[...]
    for pair in ((b0, b1), (b2, b3)):
        block = jnp.concatenate([pair[0][...], pair[1][...]], axis=0)
        acc += weighted(sharp[0], offset[0], emb[...], block, False)
    return acc


def far_kernel(sharp, offset, emb, total, b0, b1, b2, b3, out):
    out[...] = far_sum(sharp, offset, emb, total, b0, b1, b2, b3)


def last_kernel(sharp, offset, emb, total, b0, b1, b2, b3, unit, inv, theirs, out, packed):
    grad = sharp[0] * far_sum(sharp, offset, emb, total, b0, b1, b2, b3)
    text_unit = unit[...]
    inner = jnp.sum(text_unit * grad, axis=-1, keepdims=True)
    raw = (inv[:, :1] * (grad - text_unit * inner)).astype(BF16)
    out[...] = raw
    packed[:256] = raw
    for k in range(3):
        packed[256:, 256 * k : 256 * k + 256] = theirs[192 * k : 192 * k + 192]


def term_kernel(mine, raw, other, out, term):
    term[...] = jnp.dot(mine[...], raw[...], preferred_element_type=F32)
    for k in range(3):
        columns = other[256:, 256 * k : 256 * k + 256]
        term[192 * k : 192 * k + 192] += jnp.dot(columns, other[:256], preferred_element_type=F32)
    low = lax.broadcasted_iota(jnp.int32, (72, 128), 1) < 64
    pad = jnp.zeros((8, 128), F32)
    for y in range(4):
        rows = 144 * y
        for k in range(2):
            middle = 384 * k + 128
            a = term[rows : rows + 72, middle : middle + 128]
            b = term[rows + 72 : rows + 144, middle : middle + 128]
            even = jnp.where(low, a, pltpu.roll(b, 64, 1))
            odd = jnp.where(low, pltpu.roll(a, 64, 1), b)
            for x, main, rest in ((2 * k, 384 * k, even), (2 * k + 1, 384 * k + 256, odd)):
                out[4 * y + x, 0:144, :] = term[rows : rows + 144, main : main + 128].astype(BF16)
                out[4 * y + x, 144:224, :] = jnp.concatenate([rest, pad], axis=0).astype(BF16)


def local(
    visual_tower_outputs,
    language_tower_outputs,
    visual_mapping_frozen,
    language_mapping_learnable,
    sigmoid_sharpness_array,
    sigmoid_offset_array,
):
    rows, feat = language_tower_outputs.shape
    width = visual_mapping_frozen.shape[1]
    ny, nzl, nc, nx, nzh = SIZES
    devices = ny * nzl * nc * nx * nzh
    piece_r = feat // (ny * nzl * nc)
    piece_c = width // (nx * nzh)
    core = lax.axis_index("c")
    scalars = (sigmoid_sharpness_array, sigmoid_offset_array)
    part = rows // 2
    dots = 2 * rows * rows * width

    def shape(*dims, kind=BF16):
        return jax.ShapeDtypeStruct(dims, kind)

    whole, first, second = call(
        video_kernel,
        [shape(rows, width), shape(part, width), shape(part, width)],
        [pl.BlockSpec(memory_space=pl.ANY)] * 2,
        2 * rows * feat * width,
        scratch=[
            pltpu.VMEM((rows, feat), BF16),
            pltpu.VMEM((feat, width), BF16),
            pltpu.SemaphoreType.DMA((9,)),
        ],
        room=56,
    )(visual_tower_outputs, visual_mapping_frozen)

    def around(block):
        return [lax.ppermute(block, "x", ring(nx, k)) for k in (1, 3, 2)]

    first = lax.ppermute(first, "zh", ring(2, 1))

    half = feat // 2
    place = lax.broadcasted_iota(jnp.int32, (half, feat), 0)
    source = lax.broadcasted_iota(jnp.int32, (half, feat), 1)
    start = (place // piece_r) * (2 * piece_r) + place % piece_r

    def columns_of(which):
        pick = (source == start + which * piece_r).astype(BF16)
        return lax.dot_general(
            pick, language_tower_outputs, NT, preferred_element_type=F32
        ).astype(BF16)

    mine = columns_of(core)
    theirs = columns_of(1 - core)
    whole, mine, theirs = lax.optimization_barrier((whole, mine, theirs))
    near = around(whole)

    second = lax.ppermute(second, "zh", ring(2, 1))
    feats, first = lax.optimization_barrier((language_tower_outputs, first))
    unit, inv, emb = call(
        text_kernel,
        [shape(rows, width, kind=F32), shape(rows, 128, kind=F32), shape(rows, width)],
        [VMEM] * 2,
        20_000_000_000,
    )(feats, language_mapping_learnable)
    first, mine, theirs, emb, near = lax.optimization_barrier((first, mine, theirs, emb, near))
    total = call(near_kernel, shape(rows, width, kind=F32), [SMEM] * 2 + [VMEM] * 5, 8 * dots)(
        *scalars, emb, whole, *near
    )
    total = call(far_kernel, shape(rows, width, kind=F32), [SMEM] * 2 + [VMEM] * 6, 4 * dots)(
        *scalars, emb, total, first, *around(first)
    )
    raw_grad, packed = call(
        last_kernel,
        [shape(rows, width), shape(rows + half // 3, width)],
        [SMEM] * 2 + [VMEM] * 9,
        4 * dots,
    )(*scalars, emb, total, second, *around(second), unit, inv, theirs)

    other = lax.ppermute(packed, "c", ring(2, 1))
    text_grad = lax.dot_general(
        raw_grad, language_mapping_learnable, NT, preferred_element_type=F32
    ).astype(BF16)
    other, text_grad = lax.optimization_barrier((other, text_grad))

    term = call(
        term_kernel,
        shape(ny * nx, 224, 128),
        [VMEM] * 3,
        4 * half * rows * width,
        scratch=[pltpu.VMEM((half, width), F32)],
    )(mine, raw_grad, other)
    term = lax.all_to_all(term, ("y", "x"), 0, 0, tiled=True)
    term = jnp.sum(term.astype(F32), axis=0)
    main = term[:144]
    rest = jnp.concatenate([term[144:216, :64], term[144:216, 64:]], axis=0)
    is_even = lax.axis_index("x") % 2 == 0
    term = jnp.where(
        is_even, jnp.concatenate([main, rest], axis=1), jnp.concatenate([rest, main], axis=1)
    ).astype(BF16)
    term = term.reshape(nzl, piece_r, nzh, piece_c).transpose(0, 2, 1, 3)
    term = term.reshape(nzl * nzh, piece_r, piece_c)
    term = lax.all_to_all(term, ("zl", "zh"), 0, 0, tiled=True)
    head_grad = jnp.sum(term.astype(F32), axis=0) / F32(devices)
    return (text_grad, head_grad)


def solution(mesh):
    fine = Mesh(mesh.devices.reshape(SIZES), AXES)
    pairs = P(("y", "zl", "c", "x", "zh"), None)
    return jax.shard_map(
        local,
        mesh=fine,
        in_specs=(pairs, pairs, P(), P(), P(), P()),
        out_specs=(pairs, P(("y", "zl", "c"), ("x", "zh"))),
        check_vma=False,
    )
```

```python
import jax
import jax.numpy as jnp
from jax import lax
from jax.experimental import pallas as pl
from jax.experimental.pallas import tpu as pltpu
from jax.sharding import Mesh, PartitionSpec as P

EPSILON = 1e-06
AXES = ("y", "zl", "c", "x", "zh")
SIZES = (4, 8, 2, 4, 2)
F32 = jnp.float32
BF16 = jnp.bfloat16
VMEM = pl.BlockSpec(memory_space=pltpu.VMEM)
SMEM = pl.BlockSpec(memory_space=pltpu.SMEM)
NT = (((1,), (1,)), ((), ()))


def ring(n, step):
    return [(i, (i + step) % n) for i in range(n)]


def call(kernel, outs, specs, flops, scratch=(), room=40):
    return pl.pallas_call(
        kernel,
        out_shape=outs,
        in_specs=specs,
        out_specs=jax.tree.map(lambda _: VMEM, outs),
        scratch_shapes=scratch,
        compiler_params=pltpu.CompilerParams(vmem_limit_bytes=room * 1024 * 1024),
        cost_estimate=pl.CostEstimate(flops=flops, bytes_accessed=4_000_000, transcendentals=0),
    )


def embed(feats, head):
    raw = jnp.dot(feats, head, preferred_element_type=F32)
    inverse = lax.rsqrt(jnp.sum(raw * raw, axis=-1, keepdims=True) + EPSILON)
    return (raw * inverse, inverse)


def video_kernel(feats, head, whole, first, second, feats_in, head_in, landed):
    pieces, depth = 6, feats.shape[1] // 3
    step = feats.shape[1] // pieces
    moves = []
    for k in range(pieces):
        rows = pl.ds(step * k, step)
        moves.append(pltpu.make_async_copy(head.at[rows], head_in.at[rows], landed.at[k]))
        if k % 2 == 0:
            lanes = pl.ds(depth * (k // 2), depth)
            moves.append(
                pltpu.make_async_copy(
                    feats.at[:, lanes], feats_in.at[:, lanes], landed.at[pieces + k // 2]
                )
            )
    for move in moves:
        move.start()
    raw = jnp.zeros(whole.shape, F32)
    for k in range(3):
        for move in moves[3 * k : 3 * k + 3]:
            move.wait()
        span = slice(depth * k, depth * k + depth)
        raw += jnp.dot(feats_in[:, span], head_in[span], preferred_element_type=F32)
    inverse = lax.rsqrt(jnp.sum(raw * raw, axis=-1, keepdims=True) + EPSILON)
    emb = (raw * inverse).astype(BF16)
    cut = first.shape[0]
    whole[...] = emb
    first[...] = emb[:cut]
    second[...] = emb[cut:]


def weighted(sharp, offset, emb, block, diagonal):
    scores = sharp * lax.dot_general(emb, block, NT, preferred_element_type=F32) + offset
    if diagonal:
        row = lax.broadcasted_iota(jnp.int32, scores.shape, 0)
        col = lax.broadcasted_iota(jnp.int32, scores.shape, 1)
        sign = jnp.where(row == col, 1.0, -1.0).astype(F32)
        weight = -sign * jax.nn.sigmoid(-sign * scores)
    else:
        weight = jax.nn.sigmoid(scores)
    return jnp.dot(weight.astype(BF16), block, preferred_element_type=F32)


def text_kernel(feats, head, unit, inv, emb):
    text_unit, text_inv = embed(feats[...], head[...])
    unit[...] = text_unit
    inv[...] = jnp.broadcast_to(text_inv, inv.shape)
    emb[...] = text_unit.astype(BF16)


def near_kernel(sharp, offset, emb, b0, b1, b2, b3, total):
    acc = weighted(sharp[0], offset[0], emb[...], b0[...], True)
    for block in (b1, b2, b3):
        acc += weighted(sharp[0], offset[0], emb[...], block[...], False)
    total[...] = acc


def far_sum(sharp, offset, emb, total, b0, b1, b2, b3):
    acc = total[...]
    for pair in ((b0, b1), (b2, b3)):
        block = jnp.concatenate([pair[0][...], pair[1][...]], axis=0)
        acc += weighted(sharp[0], offset[0], emb[...], block, False)
    return acc


def far_kernel(sharp, offset, emb, total, b0, b1, b2, b3, out):
    out[...] = far_sum(sharp, offset, emb, total, b0, b1, b2, b3)


def last_kernel(sharp, offset, emb, total, b0, b1, b2, b3, unit, inv, theirs, out, packed):
    grad = sharp[0] * far_sum(sharp, offset, emb, total, b0, b1, b2, b3)
    text_unit = unit[...]
    inner = jnp.sum(text_unit * grad, axis=-1, keepdims=True)
    raw = (inv[:, :1] * (grad - text_unit * inner)).astype(BF16)
    out[...] = raw
    packed[:256] = raw
    for k in range(3):
        packed[256:, 256 * k : 256 * k + 256] = theirs[192 * k : 192 * k + 192]


def own_kernel(mine, raw, out):
    out[...] = jnp.dot(mine[...], raw[...], preferred_element_type=F32)


def term_kernel(own, other, out, term):
    for k in range(3):
        columns = other[256:, 256 * k : 256 * k + 256]
        term[192 * k : 192 * k + 192] = own[192 * k : 192 * k + 192] + jnp.dot(
            columns, other[:256], preferred_element_type=F32
        )
    low = lax.broadcasted_iota(jnp.int32, (72, 128), 1) < 64
    pad = jnp.zeros((8, 128), F32)
    for y in range(4):
        rows = 144 * y
        for k in range(2):
            middle = 384 * k + 128
            a = term[rows : rows + 72, middle : middle + 128]
            b = term[rows + 72 : rows + 144, middle : middle + 128]
            even = jnp.where(low, a, pltpu.roll(b, 64, 1))
            odd = jnp.where(low, pltpu.roll(a, 64, 1), b)
            for x, main, rest in ((2 * k, 384 * k, even), (2 * k + 1, 384 * k + 256, odd)):
                out[4 * y + x, 0:144, :] = term[rows : rows + 144, main : main + 128].astype(BF16)
                out[4 * y + x, 144:224, :] = jnp.concatenate([rest, pad], axis=0).astype(BF16)


def local(
    visual_tower_outputs,
    language_tower_outputs,
    visual_mapping_frozen,
    language_mapping_learnable,
    sigmoid_sharpness_array,
    sigmoid_offset_array,
):
    rows, feat = language_tower_outputs.shape
    width = visual_mapping_frozen.shape[1]
    ny, nzl, nc, nx, nzh = SIZES
    devices = ny * nzl * nc * nx * nzh
    piece_r = feat // (ny * nzl * nc)
    piece_c = width // (nx * nzh)
    core = lax.axis_index("c")
    scalars = (sigmoid_sharpness_array, sigmoid_offset_array)
    part = rows // 2
    dots = 2 * rows * rows * width

    def shape(*dims, kind=BF16):
        return jax.ShapeDtypeStruct(dims, kind)

    whole, first, second = call(
        video_kernel,
        [shape(rows, width), shape(part, width), shape(part, width)],
        [pl.BlockSpec(memory_space=pl.ANY)] * 2,
        2 * rows * feat * width,
        scratch=[
            pltpu.VMEM((rows, feat), BF16),
            pltpu.VMEM((feat, width), BF16),
            pltpu.SemaphoreType.DMA((9,)),
        ],
        room=56,
    )(visual_tower_outputs, visual_mapping_frozen)

    def around(block):
        return [lax.ppermute(block, "x", ring(nx, k)) for k in (1, 3, 2)]

    first = lax.ppermute(first, "zh", ring(2, 1))

    half = feat // 2
    place = lax.broadcasted_iota(jnp.int32, (half, feat), 0)
    source = lax.broadcasted_iota(jnp.int32, (half, feat), 1)
    start = (place // piece_r) * (2 * piece_r) + place % piece_r

    def columns_of(which):
        pick = (source == start + which * piece_r).astype(BF16)
        return lax.dot_general(
            pick, language_tower_outputs, NT, preferred_element_type=F32
        ).astype(BF16)

    mine = columns_of(core)
    theirs = columns_of(1 - core)
    whole, mine, theirs = lax.optimization_barrier((whole, mine, theirs))
    near = around(whole)

    second = lax.ppermute(second, "zh", ring(2, 1))
    feats, first = lax.optimization_barrier((language_tower_outputs, first))
    unit, inv, emb = call(
        text_kernel,
        [shape(rows, width, kind=F32), shape(rows, 128, kind=F32), shape(rows, width)],
        [VMEM] * 2,
        20_000_000_000,
    )(feats, language_mapping_learnable)
    first, mine, theirs, emb, near = lax.optimization_barrier((first, mine, theirs, emb, near))
    total = call(near_kernel, shape(rows, width, kind=F32), [SMEM] * 2 + [VMEM] * 5, 8 * dots)(
        *scalars, emb, whole, *near
    )
    total = call(far_kernel, shape(rows, width, kind=F32), [SMEM] * 2 + [VMEM] * 6, 4 * dots)(
        *scalars, emb, total, first, *around(first)
    )
    raw_grad, packed = call(
        last_kernel,
        [shape(rows, width), shape(rows + half // 3, width)],
        [SMEM] * 2 + [VMEM] * 9,
        4 * dots,
    )(*scalars, emb, total, second, *around(second), unit, inv, theirs)

    other = lax.ppermute(packed, "c", ring(2, 1))
    own = call(own_kernel, shape(half, width, kind=F32), [VMEM] * 2, 2 * half * rows * width)(
        mine, raw_grad
    )
    other, own = lax.optimization_barrier((other, own))

    term = call(
        term_kernel,
        shape(ny * nx, 224, 128),
        [VMEM] * 2,
        2 * half * rows * width,
        scratch=[pltpu.VMEM((half, width), F32)],
    )(own, other)
    raw_grad, term = lax.optimization_barrier((raw_grad, term))
    text_grad = lax.dot_general(
        raw_grad, language_mapping_learnable, NT, preferred_element_type=F32
    ).astype(BF16)
    term = lax.all_to_all(term, ("y", "x"), 0, 0, tiled=True)
    term, text_grad = lax.optimization_barrier((term, text_grad))
    term = jnp.sum(term.astype(F32), axis=0)
    main = term[:144]
    rest = jnp.concatenate([term[144:216, :64], term[144:216, 64:]], axis=0)
    is_even = lax.axis_index("x") % 2 == 0
    term = jnp.where(
        is_even, jnp.concatenate([main, rest], axis=1), jnp.concatenate([rest, main], axis=1)
    ).astype(BF16)
    term = term.reshape(nzl, piece_r, nzh, piece_c).transpose(0, 2, 1, 3)
    term = term.reshape(nzl * nzh, piece_r, piece_c)
    term = lax.all_to_all(term, ("zl", "zh"), 0, 0, tiled=True)
    head_grad = jnp.sum(term.astype(F32), axis=0) / F32(devices)
    return (text_grad, head_grad)


def solution(mesh):
    fine = Mesh(mesh.devices.reshape(SIZES), AXES)
    pairs = P(("y", "zl", "c", "x", "zh"), None)
    return jax.shard_map(
        local,
        mesh=fine,
        in_specs=(pairs, pairs, P(), P(), P(), P()),
        out_specs=(pairs, P(("y", "zl", "c"), ("x", "zh"))),
        check_vma=False,
    )
```

```python
import functools

import jax
import jax.numpy as jnp
from jax import lax
from jax.experimental import pallas as pl
from jax.experimental.pallas import tpu as pltpu
from jax.sharding import Mesh, PartitionSpec as P

EPSILON = 1e-06
AXES = ("y", "zl", "c", "x", "zh")
SIZES = (4, 8, 2, 4, 2)
F32 = jnp.float32
BF16 = jnp.bfloat16
VMEM = pl.BlockSpec(memory_space=pltpu.VMEM)
SMEM = pl.BlockSpec(memory_space=pltpu.SMEM)
NT = (((1,), (1,)), ((), ()))


def ring(n, step):
    return [(i, (i + step) % n) for i in range(n)]


def call(kernel, outs, specs, flops, scratch=(), room=40):
    return pl.pallas_call(
        kernel,
        out_shape=outs,
        in_specs=specs,
        out_specs=jax.tree.map(lambda _: VMEM, outs),
        scratch_shapes=scratch,
        compiler_params=pltpu.CompilerParams(vmem_limit_bytes=room * 1024 * 1024),
        cost_estimate=pl.CostEstimate(flops=flops, bytes_accessed=4_000_000, transcendentals=0),
    )


def embed(feats, head):
    raw = jnp.dot(feats, head, preferred_element_type=F32)
    inverse = lax.rsqrt(jnp.sum(raw * raw, axis=-1, keepdims=True) + EPSILON)
    return (raw * inverse, inverse)


def video_kernel(feats, head, whole, first, second, feats_in, head_in, landed):
    pieces, depth = 6, feats.shape[1] // 3
    step = feats.shape[1] // pieces
    moves = []
    for k in range(pieces):
        rows = pl.ds(step * k, step)
        moves.append(pltpu.make_async_copy(head.at[rows], head_in.at[rows], landed.at[k]))
        if k % 2 == 0:
            lanes = pl.ds(depth * (k // 2), depth)
            moves.append(
                pltpu.make_async_copy(
                    feats.at[:, lanes], feats_in.at[:, lanes], landed.at[pieces + k // 2]
                )
            )
    for move in moves:
        move.start()
    raw = jnp.zeros(whole.shape, F32)
    for k in range(3):
        for move in moves[3 * k : 3 * k + 3]:
            move.wait()
        span = slice(depth * k, depth * k + depth)
        raw += jnp.dot(feats_in[:, span], head_in[span], preferred_element_type=F32)
    inverse = lax.rsqrt(jnp.sum(raw * raw, axis=-1, keepdims=True) + EPSILON)
    emb = (raw * inverse).astype(BF16)
    cut = first.shape[0]
    whole[...] = emb
    first[...] = emb[:cut]
    second[...] = emb[cut:]


def weighted(sharp, offset, emb, block, diagonal):
    scores = sharp * lax.dot_general(emb, block, NT, preferred_element_type=F32) + offset
    if diagonal:
        row = lax.broadcasted_iota(jnp.int32, scores.shape, 0)
        col = lax.broadcasted_iota(jnp.int32, scores.shape, 1)
        sign = jnp.where(row == col, 1.0, -1.0).astype(F32)
        weight = -sign * jax.nn.sigmoid(-sign * scores)
    else:
        weight = jax.nn.sigmoid(scores)
    return jnp.dot(weight.astype(BF16), block, preferred_element_type=F32)


def text_kernel(feats, head, unit, inv, emb):
    text_unit, text_inv = embed(feats[...], head[...])
    unit[...] = text_unit
    inv[...] = jnp.broadcast_to(text_inv, inv.shape)
    emb[...] = text_unit.astype(BF16)


def near_kernel(sharp, offset, emb, b0, b1, b2, b3, total):
    acc = weighted(sharp[0], offset[0], emb[...], b0[...], True)
    for block in (b1, b2, b3):
        acc += weighted(sharp[0], offset[0], emb[...], block[...], False)
    total[...] = acc


def far_sum(sharp, offset, emb, total, b0, b1, b2, b3):
    acc = total[...]
    for pair in ((b0, b1), (b2, b3)):
        block = jnp.concatenate([pair[0][...], pair[1][...]], axis=0)
        acc += weighted(sharp[0], offset[0], emb[...], block, False)
    return acc


def far_kernel(sharp, offset, emb, total, b0, b1, b2, b3, out):
    out[...] = far_sum(sharp, offset, emb, total, b0, b1, b2, b3)


def last_kernel(sharp, offset, emb, total, b0, b1, b2, b3, unit, inv, theirs, out, packed):
    grad = sharp[0] * far_sum(sharp, offset, emb, total, b0, b1, b2, b3)
    text_unit = unit[...]
    inner = jnp.sum(text_unit * grad, axis=-1, keepdims=True)
    raw = (inv[:, :1] * (grad - text_unit * inner)).astype(BF16)
    out[...] = raw
    packed[:256] = raw
    for k in range(3):
        packed[256:, 256 * k : 256 * k + 256] = theirs[192 * k : 192 * k + 192]


def term_kernel(mine, raw, other, out, term):
    term[...] = jnp.dot(mine[...], raw[...], preferred_element_type=F32)
    for k in range(3):
        columns = other[256:, 256 * k : 256 * k + 256]
        term[192 * k : 192 * k + 192] += jnp.dot(columns, other[:256], preferred_element_type=F32)
    low = lax.broadcasted_iota(jnp.int32, (72, 128), 1) < 64
    pad = jnp.zeros((8, 128), F32)
    for y in range(4):
        rows = 144 * y
        for k in range(2):
            middle = 384 * k + 128
            a = term[rows : rows + 72, middle : middle + 128]
            b = term[rows + 72 : rows + 144, middle : middle + 128]
            even = jnp.where(low, a, pltpu.roll(b, 64, 1))
            odd = jnp.where(low, pltpu.roll(a, 64, 1), b)
            for x, main, rest in ((2 * k, 384 * k, even), (2 * k + 1, 384 * k + 256, odd)):
                out[4 * y + x, 0:144, :] = term[rows : rows + 144, main : main + 128].astype(BF16)
                out[4 * y + x, 144:224, :] = jnp.concatenate([rest, pad], axis=0).astype(BF16)


def mean_kernel(devices, parts, out):
    acc = parts[0].astype(F32)
    for k in range(1, parts.shape[0]):
        acc += parts[k].astype(F32)
    out[...] = acc * (1.0 / devices)


def local(
    visual_tower_outputs,
    language_tower_outputs,
    visual_mapping_frozen,
    language_mapping_learnable,
    sigmoid_sharpness_array,
    sigmoid_offset_array,
):
    rows, feat = language_tower_outputs.shape
    width = visual_mapping_frozen.shape[1]
    ny, nzl, nc, nx, nzh = SIZES
    devices = ny * nzl * nc * nx * nzh
    piece_r = feat // (ny * nzl * nc)
    piece_c = width // (nx * nzh)
    core = lax.axis_index("c")
    scalars = (sigmoid_sharpness_array, sigmoid_offset_array)
    part = rows // 2
    dots = 2 * rows * rows * width

    def shape(*dims, kind=BF16):
        return jax.ShapeDtypeStruct(dims, kind)

    whole, first, second = call(
        video_kernel,
        [shape(rows, width), shape(part, width), shape(part, width)],
        [pl.BlockSpec(memory_space=pl.ANY)] * 2,
        2 * rows * feat * width,
        scratch=[
            pltpu.VMEM((rows, feat), BF16),
            pltpu.VMEM((feat, width), BF16),
            pltpu.SemaphoreType.DMA((9,)),
        ],
        room=56,
    )(visual_tower_outputs, visual_mapping_frozen)

    def around(block):
        return [lax.ppermute(block, "x", ring(nx, k)) for k in (1, 3, 2)]

    first = lax.ppermute(first, "zh", ring(2, 1))

    half = feat // 2
    place = lax.broadcasted_iota(jnp.int32, (half, feat), 0)
    source = lax.broadcasted_iota(jnp.int32, (half, feat), 1)
    start = (place // piece_r) * (2 * piece_r) + place % piece_r

    def columns_of(which):
        pick = (source == start + which * piece_r).astype(BF16)
        return lax.dot_general(
            pick, language_tower_outputs, NT, preferred_element_type=F32
        ).astype(BF16)

    mine = columns_of(core)
    theirs = columns_of(1 - core)
    whole, mine, theirs = lax.optimization_barrier((whole, mine, theirs))
    near = around(whole)

    second = lax.ppermute(second, "zh", ring(2, 1))
    feats, first = lax.optimization_barrier((language_tower_outputs, first))
    unit, inv, emb = call(
        text_kernel,
        [shape(rows, width, kind=F32), shape(rows, 128, kind=F32), shape(rows, width)],
        [VMEM] * 2,
        20_000_000_000,
    )(feats, language_mapping_learnable)
    first, mine, theirs, emb, near = lax.optimization_barrier((first, mine, theirs, emb, near))
    total = call(near_kernel, shape(rows, width, kind=F32), [SMEM] * 2 + [VMEM] * 5, 8 * dots)(
        *scalars, emb, whole, *near
    )
    total = call(far_kernel, shape(rows, width, kind=F32), [SMEM] * 2 + [VMEM] * 6, 4 * dots)(
        *scalars, emb, total, first, *around(first)
    )
    raw_grad, packed = call(
        last_kernel,
        [shape(rows, width), shape(rows + half // 3, width)],
        [SMEM] * 2 + [VMEM] * 9,
        4 * dots,
    )(*scalars, emb, total, second, *around(second), unit, inv, theirs)

    other = lax.ppermute(packed, "c", ring(2, 1))
    text_grad = lax.dot_general(
        raw_grad, language_mapping_learnable, NT, preferred_element_type=F32
    ).astype(BF16)
    other, text_grad = lax.optimization_barrier((other, text_grad))

    term = call(
        term_kernel,
        shape(ny * nx, 224, 128),
        [VMEM] * 3,
        4 * half * rows * width,
        scratch=[pltpu.VMEM((half, width), F32)],
    )(mine, raw_grad, other)
    term = lax.all_to_all(term, ("y", "x"), 0, 0, tiled=True)
    term = jnp.sum(term.astype(F32), axis=0)
    main = term[:144]
    rest = jnp.concatenate([term[144:216, :64], term[144:216, 64:]], axis=0)
    is_even = lax.axis_index("x") % 2 == 0
    term = jnp.where(
        is_even, jnp.concatenate([main, rest], axis=1), jnp.concatenate([rest, main], axis=1)
    ).astype(BF16)
    term = term.reshape(nzl, piece_r, nzh, piece_c).transpose(0, 2, 1, 3)
    term = term.reshape(nzl * nzh, piece_r, piece_c)
    term = lax.all_to_all(term, ("zl", "zh"), 0, 0, tiled=True)
    head_grad = call(
        functools.partial(mean_kernel, devices), shape(piece_r, piece_c, kind=F32), [VMEM], 1_000_000
    )(term)
    return (text_grad, head_grad)


def solution(mesh):
    fine = Mesh(mesh.devices.reshape(SIZES), AXES)
    pairs = P(("y", "zl", "c", "x", "zh"), None)
    return jax.shard_map(
        local,
        mesh=fine,
        in_specs=(pairs, pairs, P(), P(), P(), P()),
        out_specs=(pairs, P(("y", "zl", "c"), ("x", "zh"))),
        check_vma=False,
    )
```
